32 devices in a mesh: seqa: 8 (over z, y), seqb: 4 (over x, core).
Axes of the slice: x: 2, y: 2, z: 4, core: 2. Of those that a mesh axis runs over, the one named last changes fastest.
Arguments:
- query_rows: bfloat16 [8192, 768], P(('seqa', 'seqb')), may hold values from -16 to 16
- key_rows: bfloat16 [8192, 768], P(('seqa', 'seqb')), may hold values from -16 to 16
- value_rows: bfloat16 [8192, 768], P(('seqa', 'seqb')), may hold values from -5.5 to 5.5
Outputs:
- attended: bfloat16 [8192, 768], P(('seqa', 'seqb'))
The draws below stay inside these ranges and needn't reach their ends.
All inputs are finite; a program needn't handle non-finite values.
Results may differ from the reference program's by a relative error of at most 0.0028.
Values may be sent and summed in bfloat16 or wider, within the bound.
A program may use at most 64 MiB of HBM per device.

```python
import math
import jax
import jax.numpy as jnp
from jax import lax

HEADS = 12
HEAD_DIM = 64
BLOCK = 128
TOKENS = 8192
TOP_LEVEL = 5


def common_draws(key):
    shared = jax.random.truncated_normal(jax.random.fold_in(key, 1), -4.0, 4.0, (TOKENS, HEADS * HEAD_DIM), jnp.float32)
    return shared


def smooth_waves(key, salt):
    wave_key = jax.random.fold_in(key, salt)
    octave = jax.random.uniform(jax.random.fold_in(wave_key, 1), (HEADS * HEAD_DIM,), jnp.float32, 0.0, 4.0)
    phase_shift = jax.random.uniform(jax.random.fold_in(wave_key, 2), (HEADS * HEAD_DIM,), jnp.float32, 0.0, 2.0 * math.pi)
    cycles = 16.0 * jnp.exp2(-octave) / TOKENS
    places = jnp.arange(TOKENS, dtype=jnp.float32)
    return jnp.sin(2.0 * math.pi * places[:, None] * cycles[None, :] + phase_shift[None, :])


def draw_key_rows(key, part):
    shared = common_draws(key)
    wave = smooth_waves(key, 5)
    return (3.25 * shared + 3.0 * wave).astype(jnp.bfloat16)


def draw_query_rows(key, part):
    wave = smooth_waves(key, 4)
    key = jax.random.fold_in(key, 22)
    private = jax.random.truncated_normal(key, -4.0, 4.0, (TOKENS, HEADS * HEAD_DIM), jnp.float32)
    return (private + 1.2 * wave).astype(jnp.bfloat16)


def draw_value_rows(key, part):
    wave = smooth_waves(key, 6)
    key = jax.random.fold_in(key, 23)
    private = jax.random.truncated_normal(jax.random.fold_in(key, 1), -4.0, 4.0, (TOKENS, HEADS * HEAD_DIM), jnp.float32)
    return (private + 1.5 * wave).astype(jnp.bfloat16)


def setup_inputs(seed: int = 0) -> dict:
    streams_of = jax.random.split(jax.random.key(seed), 4)
    return {
        "query_rows": draw_query_rows(jax.random.fold_in(streams_of[3], 71), 0),
        "key_rows": draw_key_rows(jax.random.fold_in(streams_of[3], 71), 0),
        "value_rows": draw_value_rows(jax.random.fold_in(streams_of[3], 71), 0),
    }


LOG_TWO = math.log(2.0)
HIGHEST = lax.Precision.HIGHEST


def halve_rows(matrix):
    amount, features = matrix.shape
    paired = matrix.reshape(amount // 2, 2, features).astype(jnp.float32)
    return 0.5 * (paired[:, 0] + paired[:, 1])


def coarse_terms(queries, halves, left_keys, right_keys, left_values, right_values, left_ok, right_ok, height):
    batches, amount, features = queries.shape
    width = left_keys.shape[1]
    head_dim = features // HEADS
    query_heads = queries.reshape(batches, amount, HEADS, head_dim)
    key_heads = jnp.concatenate([left_keys, right_keys], axis=1).reshape(batches, 2 * width, HEADS, head_dim)
    value_heads = jnp.concatenate([left_values, right_values], axis=1).reshape(batches, 2 * width, HEADS, head_dim)
    scores = jnp.einsum('bqhe,bkhe->bhqk', query_heads, key_heads, precision=HIGHEST)
    logits = scores * (head_dim ** -0.5) + height * LOG_TWO
    key_half = jnp.arange(width) >= width // 2
    query_half = halves[:, :, None]
    keep_left = (query_half | jnp.logical_not(key_half)[None, None, :]) & left_ok[:, None, None]
    keep_right = (key_half[None, None, :] | jnp.logical_not(query_half)) & right_ok[:, None, None]
    allowed = jnp.concatenate([keep_left, keep_right], axis=2)[:, None]
    logits = jnp.where(allowed, logits, -jnp.inf)
    highest = jnp.max(logits, axis=3)
    weights = jnp.exp(logits - highest[..., None])
    totals = jnp.sum(weights, axis=3)
    output = jnp.einsum('bhqk,bkhe->bqhe', weights, value_heads, precision=HIGHEST)
    return (jnp.swapaxes(highest, 1, 2), jnp.swapaxes(totals, 1, 2), output)


def merge_terms(earlier, later):
    highest = jnp.maximum(earlier[0], later[0])
    scale_one = jnp.exp(earlier[0] - highest)
    scale_two = jnp.exp(later[0] - highest)
    totals = scale_one * earlier[1] + scale_two * later[1]
    output = scale_one[..., None] * earlier[2] + scale_two[..., None] * later[2]
    return (highest, totals, output)


def widen(combined):
    return tuple(jnp.repeat(part, 2, axis=0) for part in combined)


def fine_terms(queries, keys_window, values_window, left_ok, right_ok, coarse):
    per_group, amount, heads, head_dim = queries.shape
    scores = jnp.einsum('bqhe,bkhe->bhqk', queries.astype(jnp.float32), keys_window.astype(jnp.float32), precision=HIGHEST) * (head_dim ** -0.5)
    section = jnp.arange(3 * amount) // amount
    allowed = ((section != 0)[None, :] | left_ok[:, None]) & ((section != 2)[None, :] | right_ok[:, None])
    scores = jnp.where(allowed[:, None, None, :], scores, -jnp.inf)
    highest = jnp.max(scores, axis=3)
    weights = jnp.exp(scores - highest[..., None])
    totals = jnp.sum(weights, axis=3)
    rounded = lax.optimization_barrier(weights.astype(jnp.bfloat16))
    output = jnp.einsum('bhqk,bkhe->bqhe', rounded.astype(jnp.float32), values_window.astype(jnp.float32), precision=HIGHEST)
    fine = (jnp.swapaxes(highest, 1, 2), jnp.swapaxes(totals, 1, 2), output)
    widened = tuple(jnp.repeat(part, 2, axis=0).reshape((per_group, amount) + part.shape[1:]) for part in coarse)
    merged = merge_terms(fine, widened)
    result = merged[2] / merged[1][..., None]
    return result.reshape(per_group * amount, heads * head_dim).astype(jnp.bfloat16)


def reference(query_rows, key_rows, value_rows):
    features = query_rows.shape[1]
    head_dim = features // HEADS
    results = []
    current = (query_rows, key_rows, value_rows)
    for height in range(1, TOP_LEVEL + 1):
        current = tuple(halve_rows(part) for part in current)
        amount = current[0].shape[0]
        block_count = amount // BLOCK
        query_blocks = current[0].reshape(block_count, BLOCK, features)
        padding = jnp.zeros((1, BLOCK, features), jnp.float32)
        key_blocks = jnp.concatenate([padding, current[1].reshape(block_count, BLOCK, features), padding])
        value_blocks = jnp.concatenate([padding, current[2].reshape(block_count, BLOCK, features), padding])

        def one_block(block_index, query_blocks=query_blocks, key_blocks=key_blocks, value_blocks=value_blocks, block_count=block_count, height=height):
            queries = lax.dynamic_index_in_dim(query_blocks, block_index, 0)
            left_keys = lax.dynamic_index_in_dim(key_blocks, block_index, 0)
            right_keys = lax.dynamic_index_in_dim(key_blocks, block_index + 2, 0)
            left_values = lax.dynamic_index_in_dim(value_blocks, block_index, 0)
            right_values = lax.dynamic_index_in_dim(value_blocks, block_index + 2, 0)
            halves = (jnp.arange(BLOCK) >= BLOCK // 2)[None]
            level_terms = coarse_terms(queries, halves, left_keys, right_keys, left_values, right_values, (block_index > 0)[None], (block_index < block_count - 1)[None], height)
            return tuple(part[0] for part in level_terms)

        level_terms = lax.map(one_block, jnp.arange(block_count, dtype=jnp.int32))
        results.append(tuple(part.reshape((amount,) + part.shape[2:]) for part in level_terms))
    combined = results[-1]
    for level_terms in reversed(results[:-1]):
        combined = merge_terms(widen(combined), level_terms)
    block_count = TOKENS // BLOCK
    per_group = 4
    group_count = block_count // per_group
    padding = jnp.zeros((BLOCK, features), key_rows.dtype)
    key_padded = jnp.concatenate([padding, key_rows, padding])
    value_padded = jnp.concatenate([padding, value_rows, padding])

    def fine_group(group_index):
        offset_rows = group_index * (per_group * BLOCK)
        queries = lax.dynamic_slice_in_dim(query_rows, offset_rows, per_group * BLOCK, 0).reshape(per_group, BLOCK, HEADS, head_dim)
        key_part = lax.dynamic_slice_in_dim(key_padded, offset_rows, (per_group + 2) * BLOCK, 0).reshape(per_group + 2, BLOCK, HEADS, head_dim)
        value_part = lax.dynamic_slice_in_dim(value_padded, offset_rows, (per_group + 2) * BLOCK, 0).reshape(per_group + 2, BLOCK, HEADS, head_dim)
        keys_window = jnp.concatenate([key_part[:-2], key_part[1:-1], key_part[2:]], axis=1)
        values_window = jnp.concatenate([value_part[:-2], value_part[1:-1], value_part[2:]], axis=1)
        block_ids = group_index * per_group + jnp.arange(per_group, dtype=jnp.int32)
        coarse_start = group_index * (per_group * BLOCK // 2)
        coarse = tuple(lax.dynamic_slice_in_dim(part, coarse_start, per_group * BLOCK // 2, 0) for part in combined)
        return fine_terms(queries, keys_window, values_window, block_ids > 0, block_ids < block_count - 1, coarse)

    pieces = lax.map(fine_group, jnp.arange(group_count, dtype=jnp.int32))
    return pieces.reshape(TOKENS, features)
```

```python
import functools
import math

import jax
import jax.numpy as jnp
from jax import lax
from jax.experimental import pallas as pl
from jax.experimental.pallas import tpu as pltpu
from jax.sharding import PartitionSpec as P

HEADS = 12
BLOCK = 128
LANES = 128
LOG_TWO = math.log(2.0)
NEVER = -1e30
MESH = pl.DeviceIdType.MESH


class Plan:
    def __init__(self, length, features, outer, inner):
        self.length, self.features = length, features
        self.inner = inner
        self.devices = outer * inner
        self.chips = self.devices // 2
        self.top = self.devices.bit_length() - 1
        self.levels = list(range(1, self.top + 1))
        self.deep = list(range(2, self.top + 1))
        self.rows = {l: length >> l for l in self.levels}
        self.padded = {l: max(8, length >> l) for l in self.levels}
        self.offset, total = {}, 0
        for l in self.levels:
            self.offset[l] = total
            total += self.padded[l]
        self.pooled_rows = total
        self.pairs = features // LANES

    def link_type(self, l):
        return jnp.bfloat16 if self.padded[l] >= 16 else jnp.float32

    def half_chips(self, l):
        return 2**l // 8

    def blocks(self, l):
        return self.devices // 2 ** (l - 1)


def pool_matrix(rows, columns, step):
    r = lax.broadcasted_iota(jnp.int32, (rows, columns), 0)
    c = lax.broadcasted_iota(jnp.int32, (rows, columns), 1)
    return jnp.where(c // step == r, 1.0 / step, 0.0).astype(jnp.float32)


def attend(q, keys, values, bias):
    n = q.shape[0]
    w = keys.shape[0]
    first = lax.broadcasted_iota(jnp.int32, (n, LANES), 1) < LANES // 2
    zero = jnp.zeros_like(q)
    both = jnp.concatenate([jnp.where(first, q, zero), jnp.where(first, zero, q)], axis=0)
    s = lax.dot_general(
        both.astype(jnp.bfloat16), keys, (((1,), (1,)), ((), ())), preferred_element_type=jnp.float32
    )
    if bias is not None:
        if bias.shape[0] == n:
            bias = jnp.concatenate([bias, bias], axis=0)
        s = s + bias
    m = jnp.max(s, axis=1, keepdims=True)
    p = jnp.exp(s - m).astype(jnp.bfloat16)
    right = jnp.concatenate([values, jnp.ones((w, LANES), jnp.bfloat16)], axis=1)
    r = jnp.dot(p, right, preferred_element_type=jnp.float32)
    o = jnp.where(first, r[:n, :LANES], r[n:, :LANES])
    z = jnp.where(first, r[:n, LANES:], r[n:, LANES:])
    wide = jnp.where(
        first, jnp.broadcast_to(m[:n], (n, LANES)), jnp.broadcast_to(m[n:], (n, LANES))
    )
    return wide, z, o


def merge(one, two):
    top = jnp.maximum(one[0], two[0])
    a = jnp.exp(one[0] - top)
    b = jnp.exp(two[0] - top)
    return top, a * one[1] + b * two[1], a * one[2] + b * two[2]


def kernel(plan, names, *refs):
    R = dict(zip(names, refs))
    q_ref, k_ref, v_ref, out_ref = R["q"], R["k"], R["v"], R["out"]
    feats, length = plan.features, plan.length
    half = BLOCK // 2
    pos = lax.axis_index("seqa") * plan.inner + lax.axis_index("seqb")
    core = lax.rem(pos, 2)
    other = 1 - core
    chip = lax.div(pos, 2)
    has_left = pos > 0
    has_right = pos < plan.devices - 1

    def device(p):
        return (lax.div(p, plan.inner), lax.rem(p, plan.inner))

    sibling = device(2 * chip + other)

    barrier = pltpu.get_barrier_semaphore()

    def greet(i, carry):
        @pl.when(i != chip)
        def _():
            pl.semaphore_signal(barrier, inc=1, device_id=device(2 * i + core), device_id_type=MESH)

        return carry

    lax.fori_loop(0, plan.chips, greet, 0)
    pl.semaphore_signal(barrier, inc=1, device_id=sibling, device_id_type=MESH)
    far = jnp.where(core == 0, pos - 1, pos + 1)
    has_far = (far >= 0) & (far < plan.devices)

    @pl.when(has_far)
    def _():
        pl.semaphore_signal(barrier, inc=1, device_id=device(far), device_id_type=MESH)

    pool = jnp.concatenate(
        [pool_matrix(plan.padded[l], length, 2**l) for l in plan.levels], axis=0
    ).astype(jnp.bfloat16)
    R["qp"][...] = jnp.dot(pool, q_ref[...], preferred_element_type=jnp.float32) * 0.125
    for ref, at in ((k_ref, 0), (v_ref, feats)):
        pooled = jnp.dot(pool, ref[...], preferred_element_type=jnp.float32)
        for l in plan.levels:
            part = pooled[plan.offset[l] : plan.offset[l] + plan.padded[l]]
            send = R[f"send{l}"]
            send[:, at : at + feats] = part.astype(send.dtype)

    facts = {}
    for l in plan.deep:
        span = 2 ** (l - 1)
        J = lax.div(pos, span)
        b = jnp.where(lax.rem(pos, span) >= span // 2, 1, 0)
        left_ok = J > 0
        right_ok = J < plan.blocks(l) - 1
        mid_ok = jnp.where(b == 1, J, plan.blocks(l) - 1 - J) > 0
        facts[l] = (J, b, left_ok, right_ok, (left_ok, mid_ok, right_ok))
        buf = R[f"buf{l}"]
        for slot in range(3):
            @pl.when(jnp.logical_not(facts[l][4][slot]))
            def _(buf=buf, slot=slot, l=l):
                if l == 2:
                    buf[slot] = jnp.zeros(buf.shape[1:], buf.dtype)
                else:
                    for c in range(2):
                        buf[c, slot] = jnp.zeros(buf.shape[2:], buf.dtype)

    near = R["near"]

    @pl.when(jnp.logical_not(has_left))
    def _():
        R["fk"][0] = jnp.zeros((BLOCK, feats), jnp.bfloat16)
        R["fv"][0] = jnp.zeros((BLOCK, feats), jnp.bfloat16)
        near[0:half] = jnp.zeros((half, 2 * feats), jnp.bfloat16)

    @pl.when(jnp.logical_not(has_right))
    def _():
        R["fk"][1] = jnp.zeros((BLOCK, feats), jnp.bfloat16)
        R["fv"][1] = jnp.zeros((BLOCK, feats), jnp.bfloat16)
        near[3 * half :] = jnp.zeros((half, 2 * feats), jnp.bfloat16)

    pl.semaphore_wait(barrier, plan.chips + jnp.where(has_far, 1, 0))

    def remote(src, dst, send_sem, recv_sem, target):
        return pltpu.make_async_remote_copy(
            src_ref=src, dst_ref=dst, send_sem=send_sem, recv_sem=recv_sem,
            device_id=target, device_id_type=MESH,
        )

    def deep_copies(l, t, act):
        J, b, left_ok, right_ok, _ = facts[l]
        send, buf = R[f"send{l}"], R[f"buf{l}"]
        ss, rs = R[f"ss{l}"], R[f"rs{l}"]
        if l == 2:
            group, mine, a = 1, 0, core
            ok_r = right_ok
            ok_l = left_ok
        else:
            m = plan.half_chips(l)
            group = 2 * m
            mine = lax.rem(chip, m)
            a = jnp.where(t >= m, 1, 0)
            ok_r = right_ok & (a >= b)
            ok_l = left_ok & (a <= b)
        for side, ok, step in ((0, ok_r, 1), (1, ok_l, -1)):
            slot = b + side
            dst = buf.at[slot] if l == 2 else buf.at[core, slot, mine]

            @pl.when(ok)
            def _(side=side, step=step, slot=slot, dst=dst):
                target = device(2 * ((J + step) * group + t) + core)
                act(remote(send, dst, ss.at[side, t], rs.at[slot], target))

    def all_deep(act):
        for l in reversed(plan.deep):
            if l == 2:
                deep_copies(l, 0, act)
            else:
                def body(t, carry, l=l):
                    deep_copies(l, t, act)
                    return carry

                lax.fori_loop(0, 2 * plan.half_chips(l), body, 0)

    all_deep(lambda copy: copy.start())

    def neighbour_copies(act):
        send1 = R["send1"]
        fs, fr = R["fs"], R["fr"]

        @pl.when(has_right)
        def _():
            t = device(pos + 1)
            act(remote(k_ref.at[pl.ds(BLOCK, BLOCK)], R["fk"].at[0], fs.at[0], fr.at[0], t))
            act(remote(v_ref.at[pl.ds(BLOCK, BLOCK)], R["fv"].at[0], fs.at[1], fr.at[1], t))
            act(remote(send1.at[pl.ds(0, half)], near.at[pl.ds(0, half)], fs.at[2], fr.at[2], t))

        @pl.when(has_left)
        def _():
            t = device(pos - 1)
            act(remote(k_ref.at[pl.ds(0, BLOCK)], R["fk"].at[1], fs.at[3], fr.at[3], t))
            act(remote(v_ref.at[pl.ds(0, BLOCK)], R["fv"].at[1], fs.at[4], fr.at[4], t))
            act(remote(send1.at[pl.ds(half, half)], near.at[pl.ds(3 * half, half)], fs.at[5], fr.at[5], t))

    neighbour_copies(lambda copy: copy.start())

    def lanes(hp, base=0):
        return pl.ds(pl.multiple_of(base + hp * LANES, LANES), LANES)

    def own(hp, carry):
        ls = lanes(hp)
        q = q_ref[:, ls].astype(jnp.float32) * 0.125
        m, z, o = attend(q, k_ref[:, ls], v_ref[:, ls], None)
        R["fine"][0, :, ls] = m
        R["fine"][1, :, ls] = z
        R["fine"][2, :, ls] = o
        return carry

    lax.fori_loop(0, plan.pairs, own, 0, unroll=2)

    def arrived(ref, sem):
        pltpu.make_async_copy(ref, ref, sem).wait()

    def relay(l, slot):
        buf = R[f"buf{l}"]
        if l == 2:
            return remote(buf.at[slot], buf.at[slot], R["ys2"].at[slot], R["yr2"].at[slot], sibling)
        return remote(
            buf.at[core, slot], buf.at[core, slot], R[f"ys{l}"].at[slot], R[f"yr{l}"].at[slot], sibling
        )

    for l in reversed(plan.deep):
        buf = R[f"buf{l}"]
        for slot in range(3):
            ok = facts[l][4][slot]
            if l == 2:
                direct = {0: core == 0, 1: core >= 0, 2: core == 1}[slot]

                @pl.when(ok & direct)
                def _(l=l, slot=slot, buf=buf):
                    arrived(buf.at[slot], R[f"rs{l}"].at[slot])
                    if slot != 1:
                        relay(l, slot).start()
            else:
                @pl.when(ok)
                def _(l=l, slot=slot, buf=buf):
                    arrived(buf.at[core, slot], R[f"rs{l}"].at[slot])
                    relay(l, slot).start()

    @pl.when(has_left)
    def _():
        arrived(R["fk"].at[0], R["fr"].at[0])
        arrived(R["fv"].at[0], R["fr"].at[1])
        arrived(near.at[pl.ds(0, half)], R["fr"].at[2])

    @pl.when(has_right)
    def _():
        arrived(R["fk"].at[1], R["fr"].at[3])
        arrived(R["fv"].at[1], R["fr"].at[4])
        arrived(near.at[pl.ds(3 * half, half)], R["fr"].at[5])

    pool1 = pool_matrix(half, BLOCK, 2).astype(jnp.bfloat16)
    for side in range(2):
        for name, at in (("fk", 0), ("fv", feats)):
            part = jnp.dot(pool1, R[name][side], preferred_element_type=jnp.float32)
            near[half * (1 + side) : half * (2 + side), at : at + feats] = part.astype(jnp.bfloat16)

    gone_left = jnp.where(has_left, 0.0, NEVER).astype(jnp.float32)
    gone_right = jnp.where(has_right, 0.0, NEVER).astype(jnp.float32)
    row = lax.broadcasted_iota(jnp.int32, (BLOCK, 2 * BLOCK), 0)
    col = lax.broadcasted_iota(jnp.int32, (BLOCK, 2 * BLOCK), 1)
    upper = row >= half
    quarter = col // half
    hidden = (upper & (quarter == 2)) | (jnp.logical_not(upper) & (quarter == 1))
    R["bias"][...] = jnp.where(hidden, NEVER, 0.0) + jnp.where(quarter < 2, gone_left, gone_right)

    def beside(hp, carry):
        ls = lanes(hp)
        vs = lanes(hp, feats)
        fine = R["fine"]
        for side, gone in ((0, gone_left), (1, gone_right)):
            rows = slice(side * BLOCK, (side + 1) * BLOCK)
            q = q_ref[rows, ls].astype(jnp.float32) * 0.125
            m, z, o = attend(q, R["fk"][side, :, ls], R["fv"][side, :, ls], None)
            m = m + gone
            both = merge((m, z, o), (fine[0, rows, ls], fine[1, rows, ls], fine[2, rows, ls]))
            for i in range(3):
                fine[i, rows, ls] = both[i]
        m, z, o = attend(R["qp"][0:BLOCK, ls], near[:, ls], near[:, vs], R["bias"][...])
        R["first"][0, :, ls] = m + LOG_TWO
        R["first"][1, :, ls] = z
        R["first"][2, :, ls] = o
        return carry

    lax.fori_loop(0, plan.pairs, beside, 0, unroll=2)

    for l in reversed(plan.deep):
        buf = R[f"buf{l}"]
        for slot in range(3):
            ok = facts[l][4][slot]
            if l == 2:
                if slot == 1:
                    continue

                @pl.when(ok & (core == (1 if slot == 0 else 0)))
                def _(slot=slot, buf=buf):
                    arrived(buf.at[slot], R["yr2"].at[slot])
            else:
                @pl.when(ok)
                def _(l=l, slot=slot, buf=buf):
                    arrived(buf.at[other, slot], R[f"yr{l}"].at[slot])

    def deep_bias(l):
        slots = R[f"buf{l}"].shape[:-1]
        width = math.prod(slots)
        per_slot = plan.padded[l] * (1 if l == 2 else plan.half_chips(l))
        c = lax.broadcasted_iota(jnp.int32, (1, width), 1)
        slot = lax.rem(c // per_slot, 3)
        gone = [jnp.where(ok, 0.0, NEVER).astype(jnp.float32) for ok in facts[l][4]]
        bias = jnp.where(slot == 0, gone[0], jnp.where(slot == 1, gone[1], gone[2]))
        if plan.rows[l] < plan.padded[l]:
            bias = jnp.where(lax.rem(c, plan.padded[l]) < plan.rows[l], bias, NEVER)
        return bias

    def deepest(hp, carry):
        ls = lanes(hp)
        vs = lanes(hp, feats)

        def widen(l, terms):
            wide = R[f"wide{l}"]
            n = terms[0].shape[0]
            for i in range(3):
                view = wide.at[hp, i]
                view[pl.ds(0, n, stride=2), :] = terms[i]
                view[pl.ds(1, n, stride=2), :] = terms[i]
            keep = length if l == 1 else plan.padded[l - 1]
            return tuple(wide[hp, i][:keep] for i in range(3))

        current = None
        for l in reversed(plan.levels):
            if l == 1:
                terms = tuple(R["first"][i, :, ls] for i in range(3))
            else:
                buf = R[f"buf{l}"]
                width = math.prod(buf.shape[:-1])
                at = (slice(None),) * (len(buf.shape) - 1)
                keys = buf[at + (ls,)].reshape(width, LANES).astype(jnp.bfloat16)
                values = buf[at + (vs,)].reshape(width, LANES).astype(jnp.bfloat16)
                q = R["qp"][plan.offset[l] : plan.offset[l] + plan.padded[l], ls]
                m, z, o = attend(q, keys, values, deep_bias(l))
                terms = (m + l * LOG_TWO, z, o)
            current = terms if current is None else merge(current, terms)
            current = widen(l, current)
        fine = tuple(R["fine"][i, :, ls] for i in range(3))
        _, z, o = merge(current, fine)
        out_ref[:, ls] = (o / z).astype(jnp.bfloat16)
        return carry

    lax.fori_loop(0, plan.pairs, deepest, 0, unroll=2)

    all_deep(lambda copy: copy.wait_send())
    neighbour_copies(lambda copy: copy.wait_send())
    for l in plan.deep:
        for slot in range(3):
            ok = facts[l][4][slot]
            if l == 2:
                if slot == 1:
                    continue
                ok = ok & (core == (0 if slot == 0 else 1))

            @pl.when(ok)
            def _(l=l, slot=slot):
                relay(l, slot).wait_send()


def shards(plan, q, k, v):
    f, length = plan.features, plan.length
    scratch = {}
    scratch["qp"] = pltpu.VMEM((plan.pooled_rows, f), jnp.float32)
    for l in plan.levels:
        kind = plan.link_type(l)
        scratch[f"send{l}"] = pltpu.VMEM((plan.padded[l], 2 * f), kind)
        if l == 1:
            continue
        sem = pltpu.SemaphoreType.DMA
        if l == 2:
            scratch["buf2"] = pltpu.VMEM((3, plan.padded[2], 2 * f), kind)
            scratch["ss2"] = sem((2, 1))
        else:
            m = plan.half_chips(l)
            scratch[f"buf{l}"] = pltpu.VMEM((2, 3, m, plan.padded[l], 2 * f), kind)
            scratch[f"ss{l}"] = sem((2, 2 * m))
        scratch[f"rs{l}"] = sem((3,))
        scratch[f"ys{l}"] = sem((3,))
        scratch[f"yr{l}"] = sem((3,))
    scratch["fk"] = pltpu.VMEM((2, BLOCK, f), jnp.bfloat16)
    scratch["fv"] = pltpu.VMEM((2, BLOCK, f), jnp.bfloat16)
    scratch["near"] = pltpu.VMEM((2 * BLOCK, 2 * f), jnp.bfloat16)
    scratch["fs"] = pltpu.SemaphoreType.DMA((6,))
    scratch["fr"] = pltpu.SemaphoreType.DMA((6,))
    scratch["fine"] = pltpu.VMEM((3, length, f), jnp.float32)
    scratch["first"] = pltpu.VMEM((3, BLOCK, f), jnp.float32)
    scratch["bias"] = pltpu.VMEM((BLOCK, 2 * BLOCK), jnp.float32)
    for l in plan.levels:
        scratch[f"wide{l}"] = pltpu.VMEM((plan.pairs, 3, 2 * plan.padded[l], LANES), jnp.float32)
    names = ["q", "k", "v", "out"] + list(scratch)
    return pl.pallas_call(
        functools.partial(kernel, plan, names),
        out_shape=jax.ShapeDtypeStruct((length, f), jnp.bfloat16),
        in_specs=[pl.BlockSpec(memory_space=pltpu.VMEM)] * 3,
        out_specs=pl.BlockSpec(memory_space=pltpu.VMEM),
        scratch_shapes=list(scratch.values()),
        compiler_params=pltpu.CompilerParams(
            collective_id=0, has_side_effects=True, vmem_limit_bytes=56 * 2**20
        ),
        name="hier_attention",
    )(q, k, v)


def solution(mesh):
    outer, inner = mesh.shape["seqa"], mesh.shape["seqb"]
    spec = P(("seqa", "seqb"), None)

    def part(q, k, v):
        plan = Plan(q.shape[0], q.shape[1], outer, inner)
        return shards(plan, q, k, v)

    return jax.shard_map(part, mesh=mesh, in_specs=(spec,) * 3, out_specs=spec, check_vma=False)
```

```python
import functools
import math

import jax
import jax.numpy as jnp
from jax import lax
from jax.experimental import pallas as pl
from jax.experimental.pallas import tpu as pltpu
from jax.sharding import PartitionSpec as P

HEADS = 12
BLOCK = 128
LANES = 128
LOG_TWO = math.log(2.0)
NEVER = -1e30
MESH = pl.DeviceIdType.MESH


class Plan:
    def __init__(self, length, features, outer, inner):
        self.length, self.features = length, features
        self.inner = inner
        self.devices = outer * inner
        self.chips = self.devices // 2
        self.top = self.devices.bit_length() - 1
        self.levels = list(range(1, self.top + 1))
        self.deep = list(range(2, self.top + 1))
        self.rows = {l: length >> l for l in self.levels}
        self.padded = {l: max(8, length >> l) for l in self.levels}
        self.offset, total = {}, 0
        for l in self.levels:
            self.offset[l] = total
            total += self.padded[l]
        self.pooled_rows = total
        self.pairs = features // LANES

    def packed(self, l):
        return self.padded[l] < 16

    def link_shape(self, l):
        if self.packed(l):
            return (16, self.features)
        return (self.padded[l], 2 * self.features)

    def half_chips(self, l):
        return 2**l // 8

    def blocks(self, l):
        return self.devices // 2 ** (l - 1)


def pool_matrix(rows, columns, step):
    r = lax.broadcasted_iota(jnp.int32, (rows, columns), 0)
    c = lax.broadcasted_iota(jnp.int32, (rows, columns), 1)
    return jnp.where(c // step == r, 1.0 / step, 0.0).astype(jnp.float32)


def attend(q, keys, values, bias):
    n = q.shape[0]
    w = keys.shape[0]
    first = lax.broadcasted_iota(jnp.int32, (n, LANES), 1) < LANES // 2
    zero = jnp.zeros_like(q)
    both = jnp.concatenate([jnp.where(first, q, zero), jnp.where(first, zero, q)], axis=0)
    s = lax.dot_general(
        both.astype(jnp.bfloat16), keys, (((1,), (1,)), ((), ())), preferred_element_type=jnp.float32
    )
    if bias is not None:
        if bias.shape[0] == n:
            bias = jnp.concatenate([bias, bias], axis=0)
        s = s + bias
    m = jnp.max(s, axis=1, keepdims=True)
    p = jnp.exp(s - m).astype(jnp.bfloat16)
    right = jnp.concatenate([values, jnp.ones((w, LANES), jnp.bfloat16)], axis=1)
    r = jnp.dot(p, right, preferred_element_type=jnp.float32)
    o = jnp.where(first, r[:n, :LANES], r[n:, :LANES])
    z = jnp.where(first, r[:n, LANES:], r[n:, LANES:])
    wide = jnp.where(
        first, jnp.broadcast_to(m[:n], (n, LANES)), jnp.broadcast_to(m[n:], (n, LANES))
    )
    return wide, z, o


def merge(one, two):
    top = jnp.maximum(one[0], two[0])
    a = jnp.exp(one[0] - top)
    b = jnp.exp(two[0] - top)
    return top, a * one[1] + b * two[1], a * one[2] + b * two[2]


def kernel(plan, names, *refs):
    R = dict(zip(names, refs))
    q_ref, k_ref, v_ref, out_ref = R["q"], R["k"], R["v"], R["out"]
    feats, length = plan.features, plan.length
    half = BLOCK // 2
    pos = lax.axis_index("seqa") * plan.inner + lax.axis_index("seqb")
    core = lax.rem(pos, 2)
    other = 1 - core
    chip = lax.div(pos, 2)
    has_left = pos > 0
    has_right = pos < plan.devices - 1

    def device(p):
        return (lax.div(p, plan.inner), lax.rem(p, plan.inner))

    sibling = device(2 * chip + other)

    barrier = pltpu.get_barrier_semaphore()

    def greet(i, carry):
        @pl.when(i != chip)
        def _():
            pl.semaphore_signal(barrier, inc=1, device_id=device(2 * i + core), device_id_type=MESH)

        return carry

    lax.fori_loop(0, plan.chips, greet, 0)
    pl.semaphore_signal(barrier, inc=1, device_id=sibling, device_id_type=MESH)
    far = jnp.where(core == 0, pos - 1, pos + 1)
    has_far = (far >= 0) & (far < plan.devices)

    @pl.when(has_far)
    def _():
        pl.semaphore_signal(barrier, inc=1, device_id=device(far), device_id_type=MESH)

    facts = {}
    for l in plan.deep:
        span = 2 ** (l - 1)
        J = lax.div(pos, span)
        b = jnp.where(lax.rem(pos, span) >= span // 2, 1, 0)
        left_ok = J > 0
        right_ok = J < plan.blocks(l) - 1
        mid_ok = jnp.where(b == 1, J, plan.blocks(l) - 1 - J) > 0
        facts[l] = (J, b, left_ok, right_ok, (left_ok, mid_ok, right_ok))
        buf = R[f"buf{l}"]
        for slot in range(3):
            @pl.when(jnp.logical_not(facts[l][4][slot]))
            def _(buf=buf, slot=slot, l=l):
                if l == 2:
                    buf[slot] = jnp.zeros(buf.shape[1:], buf.dtype)
                else:
                    for c in range(2):
                        buf[c, slot] = jnp.zeros(buf.shape[2:], buf.dtype)

    near = R["near"]

    @pl.when(jnp.logical_not(has_left))
    def _():
        R["fk"][0] = jnp.zeros((BLOCK, feats), jnp.bfloat16)
        R["fv"][0] = jnp.zeros((BLOCK, feats), jnp.bfloat16)
        near[0:half] = jnp.zeros((half, 2 * feats), jnp.bfloat16)

    @pl.when(jnp.logical_not(has_right))
    def _():
        R["fk"][1] = jnp.zeros((BLOCK, feats), jnp.bfloat16)
        R["fv"][1] = jnp.zeros((BLOCK, feats), jnp.bfloat16)
        near[3 * half :] = jnp.zeros((half, 2 * feats), jnp.bfloat16)

    pl.semaphore_wait(barrier, plan.chips + jnp.where(has_far, 1, 0))

    def remote(src, dst, send_sem, recv_sem, target):
        return pltpu.make_async_remote_copy(
            src_ref=src, dst_ref=dst, send_sem=send_sem, recv_sem=recv_sem,
            device_id=target, device_id_type=MESH,
        )

    def neighbour_copies(act, which):
        send1 = R["send1"]
        fs, fr = R["fs"], R["fr"]
        for side, ok, step in ((0, has_right, 1), (1, has_left, -1)):
            @pl.when(ok)
            def _(side=side, step=step):
                t = device(pos + step)
                base = 3 * side
                for i in which:
                    if i < 2:
                        src = (k_ref, v_ref)[i].at[pl.ds(BLOCK * (1 - side), BLOCK)]
                        dst = R[("fk", "fv")[i]].at[side]
                    else:
                        src = send1.at[pl.ds(half * side, half)]
                        dst = near.at[pl.ds(3 * half * side, half)]
                    act(remote(src, dst, fs.at[base + i], fr.at[base + i], t))

    neighbour_copies(lambda copy: copy.start(), (0, 1))

    pool = jnp.concatenate(
        [pool_matrix(plan.padded[l], length, 2**l) for l in plan.levels], axis=0
    ).astype(jnp.bfloat16)
    R["qp"][...] = jnp.dot(pool, q_ref[...], preferred_element_type=jnp.float32) * 0.125
    tops = {}
    for ref, at in ((k_ref, 0), (v_ref, feats)):
        pooled = jnp.dot(pool, ref[...], preferred_element_type=jnp.float32)
        for l in plan.levels:
            part = pooled[plan.offset[l] : plan.offset[l] + plan.padded[l]]
            send = R[f"send{l}"]
            if plan.packed(l):
                tops.setdefault(l, []).append(part)
            else:
                send[:, at : at + feats] = part.astype(jnp.bfloat16)
    for l, parts in tops.items():
        R[f"send{l}"][...] = jnp.concatenate(parts, axis=0).astype(jnp.bfloat16)

    neighbour_copies(lambda copy: copy.start(), (2,))

    def deep_copies(l, t, act):
        J, b, left_ok, right_ok, _ = facts[l]
        send, buf = R[f"send{l}"], R[f"buf{l}"]
        ss, rs = R[f"ss{l}"], R[f"rs{l}"]
        if l == 2:
            group, mine, a = 1, 0, core
            ok_r = right_ok & (core == 0)
            ok_l = left_ok & (core == 1)
        else:
            m = plan.half_chips(l)
            group = 2 * m
            mine = lax.rem(chip, m)
            a = jnp.where(t >= m, 1, 0)
            ok_r = right_ok & (a >= b)
            ok_l = left_ok & (a <= b)
        for side, ok, step in ((0, ok_r, 1), (1, ok_l, -1)):
            slot = b + side
            dst = buf.at[slot] if l == 2 else buf.at[core, slot, mine]

            @pl.when(ok)
            def _(side=side, step=step, slot=slot, dst=dst):
                target = device(2 * ((J + step) * group + t) + core)
                act(remote(send, dst, ss.at[side, t], rs.at[slot], target))

    def all_deep(act):
        for l in reversed(plan.deep):
            if l == 2:
                deep_copies(l, 0, act)
            else:
                def body(t, carry, l=l):
                    deep_copies(l, t, act)
                    return carry

                lax.fori_loop(0, 2 * plan.half_chips(l), body, 0)

    all_deep(lambda copy: copy.start())

    def lanes(hp, base=0):
        return pl.ds(pl.multiple_of(base + hp * LANES, LANES), LANES)

    def own(hp, carry):
        ls = lanes(hp)
        q = q_ref[:, ls].astype(jnp.float32) * 0.125
        m, z, o = attend(q, k_ref[:, ls], v_ref[:, ls], None)
        R["fine"][0, :, ls] = m
        R["fine"][1, :, ls] = z
        R["fine"][2, :, ls] = o
        return carry

    lax.fori_loop(0, plan.pairs, own, 0, unroll=2)

    def arrived(ref, sem):
        pltpu.make_async_copy(ref, ref, sem).wait()

    def relay(l, slot):
        buf = R[f"buf{l}"]
        ys, yr = R[f"ys{l}"].at[slot], R[f"yr{l}"].at[slot]
        if l == 2:
            src = R["stage"] if slot == 1 else buf.at[slot]
            return remote(src, buf.at[slot], ys, yr, sibling)
        return remote(buf.at[core, slot], buf.at[core, slot], ys, yr, sibling)

    def relays_out(l):
        ok = facts[l][4]
        if l == 2:
            return ((0, ok[0] & (core == 0)), (1, has_far), (2, ok[2] & (core == 1)))
        return tuple((slot, ok[slot]) for slot in range(3))

    def relays_in(l):
        ok = facts[l][4]
        if l == 2:
            return ((0, ok[0] & (core == 1)), (1, ok[1]), (2, ok[2] & (core == 0)))
        return tuple((slot, ok[slot]) for slot in range(3))

    def pass_on(l):
        buf = R[f"buf{l}"]
        for slot, ok in relays_out(l):
            if l == 2 and slot == 1:
                continue

            @pl.when(ok)
            def _(slot=slot):
                mine = buf.at[slot] if l == 2 else buf.at[core, slot]
                arrived(mine, R[f"rs{l}"].at[slot])
                relay(l, slot).start()

    def received(l):
        buf = R[f"buf{l}"]
        for slot, ok in relays_in(l):
            @pl.when(ok)
            def _(slot=slot):
                theirs = buf.at[slot] if l == 2 else buf.at[other, slot]
                arrived(theirs, R[f"yr{l}"].at[slot])

    @pl.when(has_left)
    def _():
        arrived(R["fk"].at[0], R["fr"].at[0])
        arrived(R["fv"].at[0], R["fr"].at[1])
        arrived(near.at[pl.ds(0, half)], R["fr"].at[2])

    @pl.when(has_right)
    def _():
        arrived(R["fk"].at[1], R["fr"].at[3])
        arrived(R["fv"].at[1], R["fr"].at[4])
        arrived(near.at[pl.ds(3 * half, half)], R["fr"].at[5])

    pool1 = pool_matrix(half, BLOCK, 2).astype(jnp.bfloat16)
    for side in range(2):
        for name, at in (("fk", 0), ("fv", feats)):
            part = jnp.dot(pool1, R[name][side], preferred_element_type=jnp.float32)
            near[half * (1 + side) : half * (2 + side), at : at + feats] = part.astype(jnp.bfloat16)

    near_at = pl.ds(pl.multiple_of(core * 3 * half, half), half)
    quart = half // 2
    pool4 = pool_matrix(quart, BLOCK, 4).astype(jnp.bfloat16)
    pool2 = pool_matrix(quart, half, 2).astype(jnp.bfloat16)
    for name, at in (("fk", 0), ("fv", feats)):
        fine_part = jnp.dot(pool4, R[name][core], preferred_element_type=jnp.float32)
        near_part = jnp.dot(pool2, near[near_at, at : at + feats], preferred_element_type=jnp.float32)
        for part, place in ((near_part, core), (fine_part, other)):
            rows = pl.ds(pl.multiple_of(place * quart, quart), quart)
            R["stage"][rows, at : at + feats] = part.astype(jnp.bfloat16)

    @pl.when(has_far)
    def _():
        relay(2, 1).start()

    gone_left = jnp.where(has_left, 0.0, NEVER).astype(jnp.float32)
    gone_right = jnp.where(has_right, 0.0, NEVER).astype(jnp.float32)
    row = lax.broadcasted_iota(jnp.int32, (BLOCK, 2 * BLOCK), 0)
    col = lax.broadcasted_iota(jnp.int32, (BLOCK, 2 * BLOCK), 1)
    upper = row >= half
    quarter = col // half
    hidden = (upper & (quarter == 2)) | (jnp.logical_not(upper) & (quarter == 1))
    R["bias"][...] = jnp.where(hidden, NEVER, 0.0) + jnp.where(quarter < 2, gone_left, gone_right)

    def beside(hp, carry):
        ls = lanes(hp)
        vs = lanes(hp, feats)
        fine = R["fine"]
        for side, gone in ((0, gone_left), (1, gone_right)):
            rows = slice(side * BLOCK, (side + 1) * BLOCK)
            q = q_ref[rows, ls].astype(jnp.float32) * 0.125
            m, z, o = attend(q, R["fk"][side, :, ls], R["fv"][side, :, ls], None)
            m = m + gone
            both = merge((m, z, o), (fine[0, rows, ls], fine[1, rows, ls], fine[2, rows, ls]))
            for i in range(3):
                fine[i, rows, ls] = both[i]
        m, z, o = attend(R["qp"][0:BLOCK, ls], near[:, ls], near[:, vs], R["bias"][...])
        R["terms1"][0, :, ls] = m + LOG_TWO
        R["terms1"][1, :, ls] = z
        R["terms1"][2, :, ls] = o
        return carry

    lax.fori_loop(0, plan.pairs, beside, 0, unroll=2)

    def key_count(l):
        return 3 * plan.padded[l] * (1 if l == 2 else 2 * plan.half_chips(l))

    def deep_bias(l):
        width = key_count(l)
        per_slot = plan.padded[l] * (1 if l == 2 else plan.half_chips(l))
        c = lax.broadcasted_iota(jnp.int32, (1, width), 1)
        slot = lax.rem(c // per_slot, 3)
        gone = [jnp.where(ok, 0.0, NEVER).astype(jnp.float32) for ok in facts[l][4]]
        bias = jnp.where(slot == 0, gone[0], jnp.where(slot == 1, gone[1], gone[2]))
        if plan.rows[l] < plan.padded[l]:
            bias = jnp.where(lax.rem(c, plan.padded[l]) < plan.rows[l], bias, NEVER)
        return bias

    def deep_level(l):
        bias = deep_bias(l)
        buf = R[f"buf{l}"]
        width = key_count(l)
        at = (slice(None),) * (len(buf.shape) - 1)

        def body(hp, carry):
            ls = lanes(hp)
            if plan.packed(l):
                block = buf[at + (ls,)].astype(jnp.float32)
                keys = block[:, :, :, :8].reshape(width, LANES).astype(jnp.bfloat16)
                values = block[:, :, :, 8:].reshape(width, LANES).astype(jnp.bfloat16)
            else:
                keys = buf[at + (ls,)].reshape(width, LANES)
                values = buf[at + (lanes(hp, feats),)].reshape(width, LANES)
            q = R["qp"][plan.offset[l] : plan.offset[l] + plan.padded[l], ls]
            m, z, o = attend(q, keys, values, bias)
            R[f"terms{l}"][0, :, ls] = m + l * LOG_TWO
            R[f"terms{l}"][1, :, ls] = z
            R[f"terms{l}"][2, :, ls] = o
            return carry

        lax.fori_loop(0, plan.pairs, body, 0, unroll=2)

    for l in reversed(plan.deep):
        pass_on(l)
    for l in reversed(plan.deep):
        received(l)
        deep_level(l)

    def last(hp, carry):
        ls = lanes(hp)

        def widen(l, terms):
            wide = R[f"wide{l}"]
            n = terms[0].shape[0]
            for i in range(3):
                view = wide.at[hp, i]
                view[pl.ds(0, n, stride=2), :] = terms[i]
                view[pl.ds(1, n, stride=2), :] = terms[i]
            keep = length if l == 1 else plan.padded[l - 1]
            return tuple(wide[hp, i][:keep] for i in range(3))

        current = None
        for l in reversed(plan.levels):
            terms = tuple(R[f"terms{l}"][i, :, ls] for i in range(3))
            current = terms if current is None else merge(current, terms)
            current = widen(l, current)
        fine = tuple(R["fine"][i, :, ls] for i in range(3))
        _, z, o = merge(current, fine)
        out_ref[:, ls] = (o / z).astype(jnp.bfloat16)
        return carry

    lax.fori_loop(0, plan.pairs, last, 0, unroll=2)

    all_deep(lambda copy: copy.wait_send())
    neighbour_copies(lambda copy: copy.wait_send(), (0, 1, 2))
    for l in plan.deep:
        for slot, ok in relays_out(l):
            @pl.when(ok)
            def _(l=l, slot=slot):
                relay(l, slot).wait_send()


def shards(plan, q, k, v):
    f, length = plan.features, plan.length
    scratch = {}
    scratch["qp"] = pltpu.VMEM((plan.pooled_rows, f), jnp.float32)
    sem = pltpu.SemaphoreType.DMA
    for l in plan.levels:
        link = plan.link_shape(l)
        scratch[f"send{l}"] = pltpu.VMEM(link, jnp.bfloat16)
        scratch[f"terms{l}"] = pltpu.VMEM((3, plan.padded[l], f), jnp.float32)
        if l == 1:
            continue
        if l == 2:
            scratch["buf2"] = pltpu.VMEM((3,) + link, jnp.bfloat16)
            scratch["stage"] = pltpu.VMEM(link, jnp.bfloat16)
            scratch["ss2"] = sem((2, 1))
        else:
            m = plan.half_chips(l)
            scratch[f"buf{l}"] = pltpu.VMEM((2, 3, m) + link, jnp.bfloat16)
            scratch[f"ss{l}"] = sem((2, 2 * m))
        scratch[f"rs{l}"] = sem((3,))
        scratch[f"ys{l}"] = sem((3,))
        scratch[f"yr{l}"] = sem((3,))
    scratch["fk"] = pltpu.VMEM((2, BLOCK, f), jnp.bfloat16)
    scratch["fv"] = pltpu.VMEM((2, BLOCK, f), jnp.bfloat16)
    scratch["near"] = pltpu.VMEM((2 * BLOCK, 2 * f), jnp.bfloat16)
    scratch["fs"] = pltpu.SemaphoreType.DMA((6,))
    scratch["fr"] = pltpu.SemaphoreType.DMA((6,))
    scratch["fine"] = pltpu.VMEM((3, length, f), jnp.float32)
    scratch["bias"] = pltpu.VMEM((BLOCK, 2 * BLOCK), jnp.float32)
    for l in plan.levels:
        scratch[f"wide{l}"] = pltpu.VMEM((plan.pairs, 3, 2 * plan.padded[l], LANES), jnp.float32)
    names = ["q", "k", "v", "out"] + list(scratch)
    return pl.pallas_call(
        functools.partial(kernel, plan, names),
        out_shape=jax.ShapeDtypeStruct((length, f), jnp.bfloat16),
        in_specs=[pl.BlockSpec(memory_space=pltpu.VMEM)] * 3,
        out_specs=pl.BlockSpec(memory_space=pltpu.VMEM),
        scratch_shapes=list(scratch.values()),
        compiler_params=pltpu.CompilerParams(
            collective_id=0, has_side_effects=True, vmem_limit_bytes=56 * 2**20
        ),
        name="hier_attention",
    )(q, k, v)


def solution(mesh):
    outer, inner = mesh.shape["seqa"], mesh.shape["seqb"]
    spec = P(("seqa", "seqb"), None)

    def part(q, k, v):
        plan = Plan(q.shape[0], q.shape[1], outer, inner)
        return shards(plan, q, k, v)

    return jax.shard_map(part, mesh=mesh, in_specs=(spec,) * 3, out_specs=spec, check_vma=False)
```

```python
import functools
import math

import jax
import jax.numpy as jnp
from jax import lax
from jax.experimental import pallas as pl
from jax.experimental.pallas import tpu as pltpu
from jax.sharding import PartitionSpec as P

HEADS = 12
BLOCK = 128
LANES = 128
LOG_TWO = math.log(2.0)
NEVER = -1e30
MESH = pl.DeviceIdType.MESH


class Plan:
    def __init__(self, length, features, outer, inner):
        self.length, self.features = length, features
        self.inner = inner
        self.devices = outer * inner
        self.chips = self.devices // 2
        self.top = self.devices.bit_length() - 1
        self.levels = list(range(1, self.top + 1))
        self.deep = list(range(2, self.top + 1))
        self.rows = {l: length >> l for l in self.levels}
        self.padded = {l: max(8, length >> l) for l in self.levels}
        self.offset, total = {}, 0
        for l in self.levels:
            self.offset[l] = total
            total += self.padded[l]
        self.pooled_rows = total
        self.pairs = features // LANES

    def packed(self, l):
        return self.padded[l] < 16

    def link_shape(self, l):
        if self.packed(l):
            return (16, self.features)
        return (self.padded[l], 2 * self.features)

    def half_chips(self, l):
        return 2**l // 8

    def blocks(self, l):
        return self.devices // 2 ** (l - 1)


def pool_matrix(rows, columns, step):
    r = lax.broadcasted_iota(jnp.int32, (rows, columns), 0)
    c = lax.broadcasted_iota(jnp.int32, (rows, columns), 1)
    return jnp.where(c // step == r, 1.0 / step, 0.0).astype(jnp.float32)


def attend(q, keys, values, bias):
    n = q.shape[0]
    w = keys.shape[0]
    first = lax.broadcasted_iota(jnp.int32, (n, LANES), 1) < LANES // 2
    zero = jnp.zeros_like(q)
    both = jnp.concatenate([jnp.where(first, q, zero), jnp.where(first, zero, q)], axis=0)
    s = lax.dot_general(
        both.astype(jnp.bfloat16), keys, (((1,), (1,)), ((), ())), preferred_element_type=jnp.float32
    )
    if bias is not None:
        if bias.shape[0] == n:
            bias = jnp.concatenate([bias, bias], axis=0)
        s = s + bias
    m = jnp.max(s, axis=1, keepdims=True)
    p = jnp.exp(s - m).astype(jnp.bfloat16)
    right = jnp.concatenate([values, jnp.ones((w, LANES), jnp.bfloat16)], axis=1)
    r = jnp.dot(p, right, preferred_element_type=jnp.float32)
    o = jnp.where(first, r[:n, :LANES], r[n:, :LANES])
    z = jnp.where(first, r[:n, LANES:], r[n:, LANES:])
    wide = jnp.where(
        first, jnp.broadcast_to(m[:n], (n, LANES)), jnp.broadcast_to(m[n:], (n, LANES))
    )
    return wide, z, o


def merge(one, two):
    top = jnp.maximum(one[0], two[0])
    a = jnp.exp(one[0] - top)
    b = jnp.exp(two[0] - top)
    return top, a * one[1] + b * two[1], a * one[2] + b * two[2]


def kernel(plan, names, *refs):
    R = dict(zip(names, refs))
    q_ref, k_ref, v_ref, out_ref = R["q"], R["k"], R["v"], R["out"]
    feats, length = plan.features, plan.length
    half = BLOCK // 2
    pos = lax.axis_index("seqa") * plan.inner + lax.axis_index("seqb")
    core = lax.rem(pos, 2)
    other = 1 - core
    chip = lax.div(pos, 2)
    has_left = pos > 0
    has_right = pos < plan.devices - 1

    def device(p):
        return (lax.div(p, plan.inner), lax.rem(p, plan.inner))

    sibling = device(2 * chip + other)

    barrier = pltpu.get_barrier_semaphore()
    bits = plan.chips.bit_length() - 1

    def across(i):
        mask = 2**i
        flipped = jnp.where(lax.rem(lax.div(chip, mask), 2) == 1, chip - mask, chip + mask)
        return device(2 * flipped + core)

    far = jnp.where(core == 0, pos - 1, pos + 1)
    has_far = (far >= 0) & (far < plan.devices)
    pl.semaphore_signal(barrier, inc=1, device_id=sibling, device_id_type=MESH)

    @pl.when(has_far)
    def _():
        pl.semaphore_signal(barrier, inc=1, device_id=device(far), device_id_type=MESH)

    for i in range(bits):
        pl.semaphore_signal(barrier, inc=1, device_id=across(i), device_id_type=MESH)

    def tell(i):
        if i < bits:
            pl.semaphore_signal(R["go"].at[i], inc=1, device_id=across(i), device_id_type=MESH)

    def hear(i):
        if i < bits:
            pl.semaphore_wait(R["go"].at[i], 1)

    facts = {}
    for l in plan.deep:
        span = 2 ** (l - 1)
        J = lax.div(pos, span)
        b = jnp.where(lax.rem(pos, span) >= span // 2, 1, 0)
        left_ok = J > 0
        right_ok = J < plan.blocks(l) - 1
        mid_ok = jnp.where(b == 1, J, plan.blocks(l) - 1 - J) > 0
        facts[l] = (J, b, left_ok, right_ok, (left_ok, mid_ok, right_ok))
        buf = R[f"buf{l}"]
        for slot in range(3):
            @pl.when(jnp.logical_not(facts[l][4][slot]))
            def _(buf=buf, slot=slot, l=l):
                if l == 2:
                    buf[slot] = jnp.zeros(buf.shape[1:], buf.dtype)
                else:
                    for c in range(2):
                        buf[c, slot] = jnp.zeros(buf.shape[2:], buf.dtype)

    near = R["near"]

    @pl.when(jnp.logical_not(has_left))
    def _():
        R["fk"][0] = jnp.zeros((BLOCK, feats), jnp.bfloat16)
        R["fv"][0] = jnp.zeros((BLOCK, feats), jnp.bfloat16)
        near[0:half] = jnp.zeros((half, 2 * feats), jnp.bfloat16)

    @pl.when(jnp.logical_not(has_right))
    def _():
        R["fk"][1] = jnp.zeros((BLOCK, feats), jnp.bfloat16)
        R["fv"][1] = jnp.zeros((BLOCK, feats), jnp.bfloat16)
        near[3 * half :] = jnp.zeros((half, 2 * feats), jnp.bfloat16)

    pl.semaphore_wait(barrier, bits + 1 + jnp.where(has_far, 1, 0))
    tell(0)

    def remote(src, dst, send_sem, recv_sem, target):
        return pltpu.make_async_remote_copy(
            src_ref=src, dst_ref=dst, send_sem=send_sem, recv_sem=recv_sem,
            device_id=target, device_id_type=MESH,
        )

    def neighbour_copies(act, which):
        send1 = R["send1"]
        fs, fr = R["fs"], R["fr"]
        for side, ok, step in ((0, has_right, 1), (1, has_left, -1)):
            @pl.when(ok)
            def _(side=side, step=step):
                t = device(pos + step)
                base = 3 * side
                for i in which:
                    if i < 2:
                        src = (k_ref, v_ref)[i].at[pl.ds(BLOCK * (1 - side), BLOCK)]
                        dst = R[("fk", "fv")[i]].at[side]
                    else:
                        src = send1.at[pl.ds(half * side, half)]
                        dst = near.at[pl.ds(3 * half * side, half)]
                    act(remote(src, dst, fs.at[base + i], fr.at[base + i], t))

    neighbour_copies(lambda copy: copy.start(), (0, 1))

    pool = jnp.concatenate(
        [pool_matrix(plan.padded[l], length, 2**l) for l in plan.levels], axis=0
    ).astype(jnp.bfloat16)
    R["qp"][...] = jnp.dot(pool, q_ref[...], preferred_element_type=jnp.float32) * 0.125
    tops = {}
    for ref, at in ((k_ref, 0), (v_ref, feats)):
        pooled = jnp.dot(pool, ref[...], preferred_element_type=jnp.float32)
        for l in plan.levels:
            part = pooled[plan.offset[l] : plan.offset[l] + plan.padded[l]]
            send = R[f"send{l}"]
            if plan.packed(l):
                tops.setdefault(l, []).append(part)
            else:
                send[:, at : at + feats] = part.astype(jnp.bfloat16)
    for l, parts in tops.items():
        R[f"send{l}"][...] = jnp.concatenate(parts, axis=0).astype(jnp.bfloat16)

    neighbour_copies(lambda copy: copy.start(), (2,))

    def lanes(hp, base=0):
        return pl.ds(pl.multiple_of(base + hp * LANES, LANES), LANES)

    def own(hp, carry):
        ls = lanes(hp)
        q = q_ref[:, ls].astype(jnp.float32) * 0.125
        m, z, o = attend(q, k_ref[:, ls], v_ref[:, ls], None)
        R["fine"][0, :, ls] = m
        R["fine"][1, :, ls] = z
        R["fine"][2, :, ls] = o
        return carry

    parts = 3
    for i in range(parts):
        hear(i)
        tell(i + 1)
        low, high = i * plan.pairs // parts, (i + 1) * plan.pairs // parts
        lax.fori_loop(low, high, own, 0, unroll=True)
    for i in range(parts, bits):
        hear(i)
        tell(i + 1)

    def deep_copies(l, t, act):
        J, b, left_ok, right_ok, _ = facts[l]
        send, buf = R[f"send{l}"], R[f"buf{l}"]
        ss, rs = R[f"ss{l}"], R[f"rs{l}"]
        if l == 2:
            group, mine, a = 1, 0, core
            ok_r = right_ok & (core == 0)
            ok_l = left_ok & (core == 1)
        else:
            m = plan.half_chips(l)
            group = 2 * m
            mine = lax.rem(chip, m)
            a = jnp.where(t >= m, 1, 0)
            ok_r = right_ok & (a >= b)
            ok_l = left_ok & (a <= b)
        for side, ok, step in ((0, ok_r, 1), (1, ok_l, -1)):
            slot = b + side
            dst = buf.at[slot] if l == 2 else buf.at[core, slot, mine]

            @pl.when(ok)
            def _(side=side, step=step, slot=slot, dst=dst):
                target = device(2 * ((J + step) * group + t) + core)
                act(remote(send, dst, ss.at[side, t], rs.at[slot], target))

    def all_deep(act):
        for l in plan.deep:
            if l == 2:
                deep_copies(l, 0, act)
            else:
                def body(t, carry, l=l):
                    deep_copies(l, t, act)
                    return carry

                lax.fori_loop(0, 2 * plan.half_chips(l), body, 0)

    all_deep(lambda copy: copy.start())

    def arrived(ref, sem):
        pltpu.make_async_copy(ref, ref, sem).wait()

    def relay(l, slot):
        buf = R[f"buf{l}"]
        ys, yr = R[f"ys{l}"].at[slot], R[f"yr{l}"].at[slot]
        if l == 2:
            src = R["stage"] if slot == 1 else buf.at[slot]
            return remote(src, buf.at[slot], ys, yr, sibling)
        return remote(buf.at[core, slot], buf.at[core, slot], ys, yr, sibling)

    def relays_out(l):
        ok = facts[l][4]
        if l == 2:
            return ((0, ok[0] & (core == 0)), (1, has_far), (2, ok[2] & (core == 1)))
        return tuple((slot, ok[slot]) for slot in range(3))

    def relays_in(l):
        ok = facts[l][4]
        if l == 2:
            return ((0, ok[0] & (core == 1)), (1, ok[1]), (2, ok[2] & (core == 0)))
        return tuple((slot, ok[slot]) for slot in range(3))

    def pass_on(l):
        buf = R[f"buf{l}"]
        for slot, ok in relays_out(l):
            if l == 2 and slot == 1:
                continue

            @pl.when(ok)
            def _(slot=slot):
                mine = buf.at[slot] if l == 2 else buf.at[core, slot]
                arrived(mine, R[f"rs{l}"].at[slot])
                relay(l, slot).start()

    def received(l):
        buf = R[f"buf{l}"]
        for slot, ok in relays_in(l):
            @pl.when(ok)
            def _(slot=slot):
                theirs = buf.at[slot] if l == 2 else buf.at[other, slot]
                arrived(theirs, R[f"yr{l}"].at[slot])

    @pl.when(has_left)
    def _():
        arrived(R["fk"].at[0], R["fr"].at[0])
        arrived(R["fv"].at[0], R["fr"].at[1])
        arrived(near.at[pl.ds(0, half)], R["fr"].at[2])

    @pl.when(has_right)
    def _():
        arrived(R["fk"].at[1], R["fr"].at[3])
        arrived(R["fv"].at[1], R["fr"].at[4])
        arrived(near.at[pl.ds(3 * half, half)], R["fr"].at[5])

    pool1 = pool_matrix(half, BLOCK, 2).astype(jnp.bfloat16)
    for side in range(2):
        for name, at in (("fk", 0), ("fv", feats)):
            part = jnp.dot(pool1, R[name][side], preferred_element_type=jnp.float32)
            near[half * (1 + side) : half * (2 + side), at : at + feats] = part.astype(jnp.bfloat16)

    near_at = pl.ds(pl.multiple_of(core * 3 * half, half), half)
    quart = half // 2
    pool4 = pool_matrix(quart, BLOCK, 4).astype(jnp.bfloat16)
    pool2 = pool_matrix(quart, half, 2).astype(jnp.bfloat16)
    for name, at in (("fk", 0), ("fv", feats)):
        fine_part = jnp.dot(pool4, R[name][core], preferred_element_type=jnp.float32)
        near_part = jnp.dot(pool2, near[near_at, at : at + feats], preferred_element_type=jnp.float32)
        for part, place in ((near_part, core), (fine_part, other)):
            rows = pl.ds(pl.multiple_of(place * quart, quart), quart)
            R["stage"][rows, at : at + feats] = part.astype(jnp.bfloat16)

    @pl.when(has_far)
    def _():
        relay(2, 1).start()

    gone_left = jnp.where(has_left, 0.0, NEVER).astype(jnp.float32)
    gone_right = jnp.where(has_right, 0.0, NEVER).astype(jnp.float32)
    row = lax.broadcasted_iota(jnp.int32, (BLOCK, 2 * BLOCK), 0)
    col = lax.broadcasted_iota(jnp.int32, (BLOCK, 2 * BLOCK), 1)
    upper = row >= half
    quarter = col // half
    hidden = (upper & (quarter == 2)) | (jnp.logical_not(upper) & (quarter == 1))
    R["bias"][...] = jnp.where(hidden, NEVER, 0.0) + jnp.where(quarter < 2, gone_left, gone_right)

    def beside(hp, carry):
        ls = lanes(hp)
        vs = lanes(hp, feats)
        fine = R["fine"]
        for side, gone in ((0, gone_left), (1, gone_right)):
            rows = slice(side * BLOCK, (side + 1) * BLOCK)
            q = q_ref[rows, ls].astype(jnp.float32) * 0.125
            m, z, o = attend(q, R["fk"][side, :, ls], R["fv"][side, :, ls], None)
            m = m + gone
            both = merge((m, z, o), (fine[0, rows, ls], fine[1, rows, ls], fine[2, rows, ls]))
            for i in range(3):
                fine[i, rows, ls] = both[i]
        m, z, o = attend(R["qp"][0:BLOCK, ls], near[:, ls], near[:, vs], R["bias"][...])
        R["terms1"][0, :, ls] = m + LOG_TWO
        R["terms1"][1, :, ls] = z
        R["terms1"][2, :, ls] = o
        return carry

    lax.fori_loop(0, plan.pairs, beside, 0, unroll=True)

    def key_count(l):
        return 3 * plan.padded[l] * (1 if l == 2 else 2 * plan.half_chips(l))

    def deep_bias(l):
        width = key_count(l)
        per_slot = plan.padded[l] * (1 if l == 2 else plan.half_chips(l))
        c = lax.broadcasted_iota(jnp.int32, (1, width), 1)
        slot = lax.rem(c // per_slot, 3)
        gone = [jnp.where(ok, 0.0, NEVER).astype(jnp.float32) for ok in facts[l][4]]
        bias = jnp.where(slot == 0, gone[0], jnp.where(slot == 1, gone[1], gone[2]))
        if plan.rows[l] < plan.padded[l]:
            bias = jnp.where(lax.rem(c, plan.padded[l]) < plan.rows[l], bias, NEVER)
        return bias

    def deep_level(l):
        bias = deep_bias(l)
        buf = R[f"buf{l}"]
        width = key_count(l)
        at = (slice(None),) * (len(buf.shape) - 1)

        def body(hp, carry):
            ls = lanes(hp)
            if plan.packed(l):
                block = buf[at + (ls,)].astype(jnp.float32)
                keys = block[:, :, :, :8].reshape(width, LANES).astype(jnp.bfloat16)
                values = block[:, :, :, 8:].reshape(width, LANES).astype(jnp.bfloat16)
            else:
                keys = buf[at + (ls,)].reshape(width, LANES)
                values = buf[at + (lanes(hp, feats),)].reshape(width, LANES)
            q = R["qp"][plan.offset[l] : plan.offset[l] + plan.padded[l], ls]
            m, z, o = attend(q, keys, values, bias)
            R[f"terms{l}"][0, :, ls] = m + l * LOG_TWO
            R[f"terms{l}"][1, :, ls] = z
            R[f"terms{l}"][2, :, ls] = o
            return carry

        lax.fori_loop(0, plan.pairs, body, 0, unroll=True)

    pass_on(plan.deep[0])
    for l in plan.deep:
        if l < plan.top:
            pass_on(l + 1)
        received(l)
        deep_level(l)

    def last(hp, carry):
        ls = lanes(hp)

        def widen(l, terms):
            wide = R[f"wide{l}"]
            n = terms[0].shape[0]
            for i in range(3):
                view = wide.at[hp, i]
                view[pl.ds(0, n, stride=2), :] = terms[i]
                view[pl.ds(1, n, stride=2), :] = terms[i]
            keep = length if l == 1 else plan.padded[l - 1]
            return tuple(wide[hp, i][:keep] for i in range(3))

        current = None
        for l in reversed(plan.levels):
            terms = tuple(R[f"terms{l}"][i, :, ls] for i in range(3))
            current = terms if current is None else merge(current, terms)
            current = widen(l, current)
        fine = tuple(R["fine"][i, :, ls] for i in range(3))
        _, z, o = merge(current, fine)
        out_ref[:, ls] = (o / z).astype(jnp.bfloat16)
        return carry

    lax.fori_loop(0, plan.pairs, last, 0, unroll=True)

    all_deep(lambda copy: copy.wait_send())
    neighbour_copies(lambda copy: copy.wait_send(), (0, 1, 2))
    for l in plan.deep:
        for slot, ok in relays_out(l):
            @pl.when(ok)
            def _(l=l, slot=slot):
                relay(l, slot).wait_send()


def shards(plan, q, k, v):
    f, length = plan.features, plan.length
    scratch = {}
    scratch["qp"] = pltpu.VMEM((plan.pooled_rows, f), jnp.float32)
    sem = pltpu.SemaphoreType.DMA
    for l in plan.levels:
        link = plan.link_shape(l)
        scratch[f"send{l}"] = pltpu.VMEM(link, jnp.bfloat16)
        scratch[f"terms{l}"] = pltpu.VMEM((3, plan.padded[l], f), jnp.float32)
        if l == 1:
            continue
        if l == 2:
            scratch["buf2"] = pltpu.VMEM((3,) + link, jnp.bfloat16)
            scratch["stage"] = pltpu.VMEM(link, jnp.bfloat16)
            scratch["ss2"] = sem((2, 1))
        else:
            m = plan.half_chips(l)
            scratch[f"buf{l}"] = pltpu.VMEM((2, 3, m) + link, jnp.bfloat16)
            scratch[f"ss{l}"] = sem((2, 2 * m))
        scratch[f"rs{l}"] = sem((3,))
        scratch[f"ys{l}"] = sem((3,))
        scratch[f"yr{l}"] = sem((3,))
    scratch["fk"] = pltpu.VMEM((2, BLOCK, f), jnp.bfloat16)
    scratch["fv"] = pltpu.VMEM((2, BLOCK, f), jnp.bfloat16)
    scratch["near"] = pltpu.VMEM((2 * BLOCK, 2 * f), jnp.bfloat16)
    scratch["go"] = pltpu.SemaphoreType.REGULAR((max(1, plan.chips.bit_length() - 1),))
    scratch["fs"] = pltpu.SemaphoreType.DMA((6,))
    scratch["fr"] = pltpu.SemaphoreType.DMA((6,))
    scratch["fine"] = pltpu.VMEM((3, length, f), jnp.float32)
    scratch["bias"] = pltpu.VMEM((BLOCK, 2 * BLOCK), jnp.float32)
    for l in plan.levels:
        scratch[f"wide{l}"] = pltpu.VMEM((plan.pairs, 3, 2 * plan.padded[l], LANES), jnp.float32)
    names = ["q", "k", "v", "out"] + list(scratch)
    return pl.pallas_call(
        functools.partial(kernel, plan, names),
        out_shape=jax.ShapeDtypeStruct((length, f), jnp.bfloat16),
        in_specs=[pl.BlockSpec(memory_space=pltpu.VMEM)] * 3,
        out_specs=pl.BlockSpec(memory_space=pltpu.VMEM),
        scratch_shapes=list(scratch.values()),
        compiler_params=pltpu.CompilerParams(
            collective_id=0, has_side_effects=True, vmem_limit_bytes=56 * 2**20
        ),
        name="hier_attention",
    )(q, k, v)


def solution(mesh):
    outer, inner = mesh.shape["seqa"], mesh.shape["seqb"]
    spec = P(("seqa", "seqb"), None)

    def part(q, k, v):
        plan = Plan(q.shape[0], q.shape[1], outer, inner)
        return shards(plan, q, k, v)

    return jax.shard_map(part, mesh=mesh, in_specs=(spec,) * 3, out_specs=spec, check_vma=False)
```

```python
import functools
import math

import jax
import jax.numpy as jnp
from jax import lax
from jax.experimental import pallas as pl
from jax.experimental.pallas import tpu as pltpu
from jax.sharding import PartitionSpec as P

HEADS = 12
BLOCK = 128
LANES = 128
LOG_TWO = math.log(2.0)
NEVER = -1e30
ALL_HEADS_ROWS = 32
MESH = pl.DeviceIdType.MESH


class Plan:
    def __init__(self, length, features, outer, inner):
        self.length, self.features = length, features
        self.inner = inner
        self.devices = outer * inner
        self.chips = self.devices // 2
        self.top = self.devices.bit_length() - 1
        self.levels = list(range(1, self.top + 1))
        self.deep = list(range(2, self.top + 1))
        self.rows = {l: length >> l for l in self.levels}
        self.padded = {l: max(8, length >> l) for l in self.levels}
        self.offset, total = {}, 0
        for l in self.levels:
            self.offset[l] = total
            total += self.padded[l]
        self.pooled_rows = total
        self.pairs = features // LANES

    def packed(self, l):
        return self.padded[l] < 16

    def link_shape(self, l):
        if self.packed(l):
            return (16, self.features)
        return (self.padded[l], 2 * self.features)

    def half_chips(self, l):
        return 2**l // 8

    def blocks(self, l):
        return self.devices // 2 ** (l - 1)


def pool_matrix(rows, columns, step):
    r = lax.broadcasted_iota(jnp.int32, (rows, columns), 0)
    c = lax.broadcasted_iota(jnp.int32, (rows, columns), 1)
    return jnp.where(c // step == r, 1.0 / step, 0.0).astype(jnp.float32)


def attend(q, keys, values, bias):
    n = q.shape[0]
    w = keys.shape[0]
    first = lax.broadcasted_iota(jnp.int32, (n, LANES), 1) < LANES // 2
    zero = jnp.zeros_like(q)
    both = jnp.concatenate([jnp.where(first, q, zero), jnp.where(first, zero, q)], axis=0)
    s = lax.dot_general(
        both.astype(jnp.bfloat16), keys, (((1,), (1,)), ((), ())), preferred_element_type=jnp.float32
    )
    if bias is not None:
        if bias.shape[0] == n:
            bias = jnp.concatenate([bias, bias], axis=0)
        s = s + bias
    m = jnp.max(s, axis=1, keepdims=True)
    p = jnp.exp(s - m).astype(jnp.bfloat16)
    right = jnp.concatenate([values, jnp.ones((w, LANES), jnp.bfloat16)], axis=1)
    r = jnp.dot(p, right, preferred_element_type=jnp.float32)
    o = jnp.where(first, r[:n, :LANES], r[n:, :LANES])
    z = jnp.where(first, r[:n, LANES:], r[n:, LANES:])
    wide = jnp.where(
        first, jnp.broadcast_to(m[:n], (n, LANES)), jnp.broadcast_to(m[n:], (n, LANES))
    )
    return wide, z, o


def attend_all(q, keys, values, bias):
    n, feats = q.shape
    w = keys.shape[0]
    head_dim = feats // HEADS
    row = lax.broadcasted_iota(jnp.int32, (HEADS * n, feats), 0)
    lane = lax.broadcasted_iota(jnp.int32, (HEADS * n, feats), 1)
    tall = jnp.concatenate([q] * HEADS, axis=0)
    tall = jnp.where(row // n == lane // head_dim, tall, 0.0).astype(jnp.bfloat16)
    s = lax.dot_general(tall, keys, (((1,), (1,)), ((), ())), preferred_element_type=jnp.float32)
    s = s + bias
    m = jnp.max(s, axis=1, keepdims=True)
    p = jnp.exp(s - m).astype(jnp.bfloat16)
    r = jnp.dot(p, values, preferred_element_type=jnp.float32)
    z = jnp.dot(p, jnp.ones((w, LANES), jnp.bfloat16), preferred_element_type=jnp.float32)
    first = lax.broadcasted_iota(jnp.int32, (n, LANES), 1) < LANES // 2
    parts = []
    for hp in range(feats // LANES):
        a = slice(2 * hp * n, (2 * hp + 1) * n)
        b = slice((2 * hp + 1) * n, (2 * hp + 2) * n)
        ls = slice(hp * LANES, (hp + 1) * LANES)
        wide = jnp.where(
            first, jnp.broadcast_to(m[a], (n, LANES)), jnp.broadcast_to(m[b], (n, LANES))
        )
        parts.append((wide, jnp.where(first, z[a], z[b]), jnp.where(first, r[a, ls], r[b, ls])))
    return parts


def merge(one, two):
    top = jnp.maximum(one[0], two[0])
    a = jnp.exp(one[0] - top)
    b = jnp.exp(two[0] - top)
    return top, a * one[1] + b * two[1], a * one[2] + b * two[2]


def kernel(plan, names, *refs):
    R = dict(zip(names, refs))
    q_ref, k_ref, v_ref, out_ref = R["q"], R["k"], R["v"], R["out"]
    feats, length = plan.features, plan.length
    half = BLOCK // 2
    pos = lax.axis_index("seqa") * plan.inner + lax.axis_index("seqb")
    core = lax.rem(pos, 2)
    other = 1 - core
    chip = lax.div(pos, 2)
    has_left = pos > 0
    has_right = pos < plan.devices - 1

    def device(p):
        return (lax.div(p, plan.inner), lax.rem(p, plan.inner))

    sibling = device(2 * chip + other)

    barrier = pltpu.get_barrier_semaphore()
    bits = plan.chips.bit_length() - 1

    def across(i):
        mask = 2**i
        flipped = jnp.where(lax.rem(lax.div(chip, mask), 2) == 1, chip - mask, chip + mask)
        return device(2 * flipped + core)

    far = jnp.where(core == 0, pos - 1, pos + 1)
    has_far = (far >= 0) & (far < plan.devices)
    pl.semaphore_signal(barrier, inc=1, device_id=sibling, device_id_type=MESH)

    @pl.when(has_far)
    def _():
        pl.semaphore_signal(barrier, inc=1, device_id=device(far), device_id_type=MESH)

    for i in range(bits):
        pl.semaphore_signal(barrier, inc=1, device_id=across(i), device_id_type=MESH)

    def tell(i):
        if i < bits:
            pl.semaphore_signal(R["go"].at[i], inc=1, device_id=across(i), device_id_type=MESH)

    def hear(i):
        if i < bits:
            pl.semaphore_wait(R["go"].at[i], 1)

    facts = {}
    for l in plan.deep:
        span = 2 ** (l - 1)
        J = lax.div(pos, span)
        b = jnp.where(lax.rem(pos, span) >= span // 2, 1, 0)
        left_ok = J > 0
        right_ok = J < plan.blocks(l) - 1
        mid_ok = jnp.where(b == 1, J, plan.blocks(l) - 1 - J) > 0
        facts[l] = (J, b, left_ok, right_ok, (left_ok, mid_ok, right_ok))
        buf = R[f"buf{l}"]
        for slot in range(3):
            @pl.when(jnp.logical_not(facts[l][4][slot]))
            def _(buf=buf, slot=slot, l=l):
                if l == 2:
                    buf[slot] = jnp.zeros(buf.shape[1:], buf.dtype)
                else:
                    for c in range(2):
                        buf[c, slot] = jnp.zeros(buf.shape[2:], buf.dtype)

    near = R["near"]

    @pl.when(jnp.logical_not(has_left))
    def _():
        R["fk"][0] = jnp.zeros((BLOCK, feats), jnp.bfloat16)
        R["fv"][0] = jnp.zeros((BLOCK, feats), jnp.bfloat16)
        near[0:half] = jnp.zeros((half, 2 * feats), jnp.bfloat16)

    @pl.when(jnp.logical_not(has_right))
    def _():
        R["fk"][1] = jnp.zeros((BLOCK, feats), jnp.bfloat16)
        R["fv"][1] = jnp.zeros((BLOCK, feats), jnp.bfloat16)
        near[3 * half :] = jnp.zeros((half, 2 * feats), jnp.bfloat16)

    pl.semaphore_wait(barrier, bits + 1 + jnp.where(has_far, 1, 0))
    tell(0)

    def remote(src, dst, send_sem, recv_sem, target):
        return pltpu.make_async_remote_copy(
            src_ref=src, dst_ref=dst, send_sem=send_sem, recv_sem=recv_sem,
            device_id=target, device_id_type=MESH,
        )

    def neighbour_copies(act, which):
        send1 = R["send1"]
        fs, fr = R["fs"], R["fr"]
        for side, ok, step in ((0, has_right, 1), (1, has_left, -1)):
            @pl.when(ok)
            def _(side=side, step=step):
                t = device(pos + step)
                base = 3 * side
                for i in which:
                    if i < 2:
                        src = (k_ref, v_ref)[i].at[pl.ds(BLOCK * (1 - side), BLOCK)]
                        dst = R[("fk", "fv")[i]].at[side]
                    else:
                        src = send1.at[pl.ds(half * side, half)]
                        dst = near.at[pl.ds(3 * half * side, half)]
                    act(remote(src, dst, fs.at[base + i], fr.at[base + i], t))

    neighbour_copies(lambda copy: copy.start(), (0, 1))

    pool = jnp.concatenate(
        [pool_matrix(plan.padded[l], length, 2**l) for l in plan.levels], axis=0
    ).astype(jnp.bfloat16)
    R["qp"][...] = jnp.dot(pool, q_ref[...], preferred_element_type=jnp.float32) * 0.125
    tops = {}
    for ref, at in ((k_ref, 0), (v_ref, feats)):
        pooled = jnp.dot(pool, ref[...], preferred_element_type=jnp.float32)
        for l in plan.levels:
            part = pooled[plan.offset[l] : plan.offset[l] + plan.padded[l]]
            send = R[f"send{l}"]
            if plan.packed(l):
                tops.setdefault(l, []).append(part)
            else:
                send[:, at : at + feats] = part.astype(jnp.bfloat16)
    for l, parts in tops.items():
        R[f"send{l}"][...] = jnp.concatenate(parts, axis=0).astype(jnp.bfloat16)

    neighbour_copies(lambda copy: copy.start(), (2,))

    def lanes(hp, base=0):
        return pl.ds(pl.multiple_of(base + hp * LANES, LANES), LANES)

    def own(hp, carry):
        ls = lanes(hp)
        q = q_ref[:, ls].astype(jnp.float32) * 0.125
        m, z, o = attend(q, k_ref[:, ls], v_ref[:, ls], None)
        R["fine"][0, :, ls] = m
        R["fine"][1, :, ls] = z
        R["fine"][2, :, ls] = o
        return carry

    parts = 3
    for i in range(parts):
        hear(i)
        tell(i + 1)
        low, high = i * plan.pairs // parts, (i + 1) * plan.pairs // parts
        lax.fori_loop(low, high, own, 0, unroll=True)
    for i in range(parts, bits):
        hear(i)
        tell(i + 1)

    def deep_copies(l, t, act):
        J, b, left_ok, right_ok, _ = facts[l]
        send, buf = R[f"send{l}"], R[f"buf{l}"]
        ss, rs = R[f"ss{l}"], R[f"rs{l}"]
        if l == 2:
            group, mine, a = 1, 0, core
            ok_r = right_ok & (core == 0)
            ok_l = left_ok & (core == 1)
        else:
            m = plan.half_chips(l)
            group = 2 * m
            mine = lax.rem(chip, m)
            a = jnp.where(t >= m, 1, 0)
            ok_r = right_ok & (a >= b)
            ok_l = left_ok & (a <= b)
        for side, ok, step in ((0, ok_r, 1), (1, ok_l, -1)):
            slot = b + side
            dst = buf.at[slot] if l == 2 else buf.at[core, slot, mine]

            @pl.when(ok)
            def _(side=side, step=step, slot=slot, dst=dst):
                target = device(2 * ((J + step) * group + t) + core)
                act(remote(send, dst, ss.at[side, t], rs.at[slot], target))

    def all_deep(act):
        for l in plan.deep:
            if l == 2:
                deep_copies(l, 0, act)
            else:
                def body(t, carry, l=l):
                    deep_copies(l, t, act)
                    return carry

                lax.fori_loop(0, 2 * plan.half_chips(l), body, 0)

    all_deep(lambda copy: copy.start())

    def arrived(ref, sem):
        pltpu.make_async_copy(ref, ref, sem).wait()

    def relay(l, slot):
        buf = R[f"buf{l}"]
        ys, yr = R[f"ys{l}"].at[slot], R[f"yr{l}"].at[slot]
        if l == 2:
            src = R["stage"] if slot == 1 else buf.at[slot]
            return remote(src, buf.at[slot], ys, yr, sibling)
        return remote(buf.at[core, slot], buf.at[core, slot], ys, yr, sibling)

    def relays_out(l):
        ok = facts[l][4]
        if l == 2:
            return ((0, ok[0] & (core == 0)), (1, has_far), (2, ok[2] & (core == 1)))
        return tuple((slot, ok[slot]) for slot in range(3))

    def relays_in(l):
        ok = facts[l][4]
        if l == 2:
            return ((0, ok[0] & (core == 1)), (1, ok[1]), (2, ok[2] & (core == 0)))
        return tuple((slot, ok[slot]) for slot in range(3))

    def pass_on(l):
        buf = R[f"buf{l}"]
        for slot, ok in relays_out(l):
            if l == 2 and slot == 1:
                continue

            @pl.when(ok)
            def _(slot=slot):
                mine = buf.at[slot] if l == 2 else buf.at[core, slot]
                arrived(mine, R[f"rs{l}"].at[slot])
                relay(l, slot).start()

    def received(l):
        buf = R[f"buf{l}"]
        for slot, ok in relays_in(l):
            @pl.when(ok)
            def _(slot=slot):
                theirs = buf.at[slot] if l == 2 else buf.at[other, slot]
                arrived(theirs, R[f"yr{l}"].at[slot])

    @pl.when(has_left)
    def _():
        arrived(R["fk"].at[0], R["fr"].at[0])
        arrived(R["fv"].at[0], R["fr"].at[1])
        arrived(near.at[pl.ds(0, half)], R["fr"].at[2])

    @pl.when(has_right)
    def _():
        arrived(R["fk"].at[1], R["fr"].at[3])
        arrived(R["fv"].at[1], R["fr"].at[4])
        arrived(near.at[pl.ds(3 * half, half)], R["fr"].at[5])

    pool1 = pool_matrix(half, BLOCK, 2).astype(jnp.bfloat16)
    for side in range(2):
        for name, at in (("fk", 0), ("fv", feats)):
            part = jnp.dot(pool1, R[name][side], preferred_element_type=jnp.float32)
            near[half * (1 + side) : half * (2 + side), at : at + feats] = part.astype(jnp.bfloat16)

    near_at = pl.ds(pl.multiple_of(core * 3 * half, half), half)
    quart = half // 2
    pool4 = pool_matrix(quart, BLOCK, 4).astype(jnp.bfloat16)
    pool2 = pool_matrix(quart, half, 2).astype(jnp.bfloat16)
    for name, at in (("fk", 0), ("fv", feats)):
        fine_part = jnp.dot(pool4, R[name][core], preferred_element_type=jnp.float32)
        near_part = jnp.dot(pool2, near[near_at, at : at + feats], preferred_element_type=jnp.float32)
        for part, place in ((near_part, core), (fine_part, other)):
            rows = pl.ds(pl.multiple_of(place * quart, quart), quart)
            R["stage"][rows, at : at + feats] = part.astype(jnp.bfloat16)

    @pl.when(has_far)
    def _():
        relay(2, 1).start()

    gone_left = jnp.where(has_left, 0.0, NEVER).astype(jnp.float32)
    gone_right = jnp.where(has_right, 0.0, NEVER).astype(jnp.float32)
    row = lax.broadcasted_iota(jnp.int32, (BLOCK, 2 * BLOCK), 0)
    col = lax.broadcasted_iota(jnp.int32, (BLOCK, 2 * BLOCK), 1)
    upper = row >= half
    quarter = col // half
    hidden = (upper & (quarter == 2)) | (jnp.logical_not(upper) & (quarter == 1))
    R["bias"][...] = jnp.where(hidden, NEVER, 0.0) + jnp.where(quarter < 2, gone_left, gone_right)

    def beside(hp, carry):
        ls = lanes(hp)
        vs = lanes(hp, feats)
        fine = R["fine"]
        for side, gone in ((0, gone_left), (1, gone_right)):
            rows = slice(side * BLOCK, (side + 1) * BLOCK)
            q = q_ref[rows, ls].astype(jnp.float32) * 0.125
            m, z, o = attend(q, R["fk"][side, :, ls], R["fv"][side, :, ls], None)
            m = m + gone
            both = merge((m, z, o), (fine[0, rows, ls], fine[1, rows, ls], fine[2, rows, ls]))
            for i in range(3):
                fine[i, rows, ls] = both[i]
        m, z, o = attend(R["qp"][0:BLOCK, ls], near[:, ls], near[:, vs], R["bias"][...])
        R["terms1"][0, :, ls] = m + LOG_TWO
        R["terms1"][1, :, ls] = z
        R["terms1"][2, :, ls] = o
        return carry

    lax.fori_loop(0, plan.pairs, beside, 0, unroll=True)

    def key_count(l):
        return 3 * plan.padded[l] * (1 if l == 2 else 2 * plan.half_chips(l))

    def deep_bias(l):
        width = key_count(l)
        per_slot = plan.padded[l] * (1 if l == 2 else plan.half_chips(l))
        c = lax.broadcasted_iota(jnp.int32, (1, width), 1)
        slot = lax.rem(c // per_slot, 3)
        gone = [jnp.where(ok, 0.0, NEVER).astype(jnp.float32) for ok in facts[l][4]]
        bias = jnp.where(slot == 0, gone[0], jnp.where(slot == 1, gone[1], gone[2]))
        if plan.rows[l] < plan.padded[l]:
            bias = jnp.where(lax.rem(c, plan.padded[l]) < plan.rows[l], bias, NEVER)
        return bias

    def deep_level(l):
        bias = deep_bias(l)
        buf = R[f"buf{l}"]
        width = key_count(l)
        at = (slice(None),) * (len(buf.shape) - 1)

        def body(hp, carry):
            ls = lanes(hp)
            if plan.packed(l):
                block = buf[at + (ls,)].astype(jnp.float32)
                keys = block[:, :, :, :8].reshape(width, LANES).astype(jnp.bfloat16)
                values = block[:, :, :, 8:].reshape(width, LANES).astype(jnp.bfloat16)
            else:
                keys = buf[at + (ls,)].reshape(width, LANES)
                values = buf[at + (lanes(hp, feats),)].reshape(width, LANES)
            q = R["qp"][plan.offset[l] : plan.offset[l] + plan.padded[l], ls]
            m, z, o = attend(q, keys, values, bias)
            R[f"terms{l}"][0, :, ls] = m + l * LOG_TWO
            R[f"terms{l}"][1, :, ls] = z
            R[f"terms{l}"][2, :, ls] = o
            return carry

        if plan.padded[l] > ALL_HEADS_ROWS:
            lax.fori_loop(0, plan.pairs, body, 0, unroll=True)
            return
        if plan.packed(l):
            block = buf[...].astype(jnp.float32)
            keys = block[:, :, :, :8].reshape(width, feats).astype(jnp.bfloat16)
            values = block[:, :, :, 8:].reshape(width, feats).astype(jnp.bfloat16)
        else:
            keys = buf[at + (slice(0, feats),)].reshape(width, feats)
            values = buf[at + (slice(feats, 2 * feats),)].reshape(width, feats)
        q = R["qp"][plan.offset[l] : plan.offset[l] + plan.padded[l], :]
        for hp, (m, z, o) in enumerate(attend_all(q, keys, values, bias)):
            ls = slice(hp * LANES, (hp + 1) * LANES)
            R[f"terms{l}"][0, :, ls] = m + l * LOG_TWO
            R[f"terms{l}"][1, :, ls] = z
            R[f"terms{l}"][2, :, ls] = o

    pass_on(plan.deep[0])
    for l in plan.deep:
        if l < plan.top:
            pass_on(l + 1)
        received(l)
        deep_level(l)

    def last(hp, carry):
        ls = lanes(hp)

        def widen(l, terms):
            wide = R[f"wide{l}"]
            n = terms[0].shape[0]
            for i in range(3):
                view = wide.at[hp, i]
                view[pl.ds(0, n, stride=2), :] = terms[i]
                view[pl.ds(1, n, stride=2), :] = terms[i]
            keep = length if l == 1 else plan.padded[l - 1]
            return tuple(wide[hp, i][:keep] for i in range(3))

        current = None
        for l in reversed(plan.levels):
            terms = tuple(R[f"terms{l}"][i, :, ls] for i in range(3))
            current = terms if current is None else merge(current, terms)
            current = widen(l, current)
        fine = tuple(R["fine"][i, :, ls] for i in range(3))
        _, z, o = merge(current, fine)
        out_ref[:, ls] = (o / z).astype(jnp.bfloat16)
        return carry

    lax.fori_loop(0, plan.pairs, last, 0, unroll=True)

    all_deep(lambda copy: copy.wait_send())
    neighbour_copies(lambda copy: copy.wait_send(), (0, 1, 2))
    for l in plan.deep:
        for slot, ok in relays_out(l):
            @pl.when(ok)
            def _(l=l, slot=slot):
                relay(l, slot).wait_send()


def shards(plan, q, k, v):
    f, length = plan.features, plan.length
    scratch = {}
    scratch["qp"] = pltpu.VMEM((plan.pooled_rows, f), jnp.float32)
    sem = pltpu.SemaphoreType.DMA
    for l in plan.levels:
        link = plan.link_shape(l)
        scratch[f"send{l}"] = pltpu.VMEM(link, jnp.bfloat16)
        scratch[f"terms{l}"] = pltpu.VMEM((3, plan.padded[l], f), jnp.float32)
        if l == 1:
            continue
        if l == 2:
            scratch["buf2"] = pltpu.VMEM((3,) + link, jnp.bfloat16)
            scratch["stage"] = pltpu.VMEM(link, jnp.bfloat16)
            scratch["ss2"] = sem((2, 1))
        else:
            m = plan.half_chips(l)
            scratch[f"buf{l}"] = pltpu.VMEM((2, 3, m) + link, jnp.bfloat16)
            scratch[f"ss{l}"] = sem((2, 2 * m))
        scratch[f"rs{l}"] = sem((3,))
        scratch[f"ys{l}"] = sem((3,))
        scratch[f"yr{l}"] = sem((3,))
    scratch["fk"] = pltpu.VMEM((2, BLOCK, f), jnp.bfloat16)
    scratch["fv"] = pltpu.VMEM((2, BLOCK, f), jnp.bfloat16)
    scratch["near"] = pltpu.VMEM((2 * BLOCK, 2 * f), jnp.bfloat16)
    scratch["go"] = pltpu.SemaphoreType.REGULAR((max(1, plan.chips.bit_length() - 1),))
    scratch["fs"] = pltpu.SemaphoreType.DMA((6,))
    scratch["fr"] = pltpu.SemaphoreType.DMA((6,))
    scratch["fine"] = pltpu.VMEM((3, length, f), jnp.float32)
    scratch["bias"] = pltpu.VMEM((BLOCK, 2 * BLOCK), jnp.float32)
    for l in plan.levels:
        scratch[f"wide{l}"] = pltpu.VMEM((plan.pairs, 3, 2 * plan.padded[l], LANES), jnp.float32)
    names = ["q", "k", "v", "out"] + list(scratch)
    return pl.pallas_call(
        functools.partial(kernel, plan, names),
        out_shape=jax.ShapeDtypeStruct((length, f), jnp.bfloat16),
        in_specs=[pl.BlockSpec(memory_space=pltpu.VMEM)] * 3,
        out_specs=pl.BlockSpec(memory_space=pltpu.VMEM),
        scratch_shapes=list(scratch.values()),
        compiler_params=pltpu.CompilerParams(
            collective_id=0, has_side_effects=True, vmem_limit_bytes=56 * 2**20
        ),
        name="hier_attention",
    )(q, k, v)


def solution(mesh):
    outer, inner = mesh.shape["seqa"], mesh.shape["seqb"]
    spec = P(("seqa", "seqb"), None)

    def part(q, k, v):
        plan = Plan(q.shape[0], q.shape[1], outer, inner)
        return shards(plan, q, k, v)

    return jax.shard_map(part, mesh=mesh, in_specs=(spec,) * 3, out_specs=spec, check_vma=False)
```

```python
import functools
import math

import jax
import jax.numpy as jnp
from jax import lax
from jax.experimental import pallas as pl
from jax.experimental.pallas import tpu as pltpu
from jax.sharding import PartitionSpec as P

HEADS = 12
BLOCK = 128
LANES = 128
LOG_TWO = math.log(2.0)
NEVER = -1e30
ALL_HEADS_ROWS = 32
MESH = pl.DeviceIdType.MESH


class Plan:
    def __init__(self, length, features, outer, inner):
        self.length, self.features = length, features
        self.inner = inner
        self.devices = outer * inner
        self.chips = self.devices // 2
        self.top = self.devices.bit_length() - 1
        self.levels = list(range(1, self.top + 1))
        self.deep = list(range(2, self.top + 1))
        self.rows = {l: length >> l for l in self.levels}
        self.padded = {l: max(8, length >> l) for l in self.levels}
        self.offset, total = {}, 0
        for l in self.levels:
            self.offset[l] = total
            total += self.padded[l]
        self.pooled_rows = total
        self.pairs = features // LANES

    def packed(self, l):
        return self.padded[l] < 16

    def link_shape(self, l):
        if self.packed(l):
            return (16, self.features)
        return (self.padded[l], 2 * self.features)

    def half_chips(self, l):
        return 2**l // 8

    def blocks(self, l):
        return self.devices // 2 ** (l - 1)


def pool_matrix(rows, columns, step):
    r = lax.broadcasted_iota(jnp.int32, (rows, columns), 0)
    c = lax.broadcasted_iota(jnp.int32, (rows, columns), 1)
    return jnp.where(c // step == r, 1.0 / step, 0.0).astype(jnp.float32)


def attend(q, keys, values, bias):
    n = q.shape[0]
    w = keys.shape[0]
    first = lax.broadcasted_iota(jnp.int32, (n, LANES), 1) < LANES // 2
    zero = jnp.zeros_like(q)
    both = jnp.concatenate([jnp.where(first, q, zero), jnp.where(first, zero, q)], axis=0)
    s = lax.dot_general(
        both.astype(jnp.bfloat16), keys, (((1,), (1,)), ((), ())), preferred_element_type=jnp.float32
    )
    if bias is not None:
        if bias.shape[0] == n:
            bias = jnp.concatenate([bias, bias], axis=0)
        s = s + bias
    m = jnp.max(s, axis=1, keepdims=True)
    p = jnp.exp(s - m).astype(jnp.bfloat16)
    right = jnp.concatenate([values, jnp.ones((w, LANES), jnp.bfloat16)], axis=1)
    r = jnp.dot(p, right, preferred_element_type=jnp.float32)
    o = jnp.where(first, r[:n, :LANES], r[n:, :LANES])
    z = jnp.where(first, r[:n, LANES:], r[n:, LANES:])
    wide = jnp.where(
        first, jnp.broadcast_to(m[:n], (n, LANES)), jnp.broadcast_to(m[n:], (n, LANES))
    )
    return wide, z, o


def attend_all(q, keys, values, bias):
    n, feats = q.shape
    w = keys.shape[0]
    head_dim = feats // HEADS
    row = lax.broadcasted_iota(jnp.int32, (HEADS * n, feats), 0)
    lane = lax.broadcasted_iota(jnp.int32, (HEADS * n, feats), 1)
    tall = jnp.concatenate([q] * HEADS, axis=0)
    tall = jnp.where(row // n == lane // head_dim, tall, 0.0).astype(jnp.bfloat16)
    s = lax.dot_general(tall, keys, (((1,), (1,)), ((), ())), preferred_element_type=jnp.float32)
    s = s + bias
    m = jnp.max(s, axis=1, keepdims=True)
    p = jnp.exp(s - m).astype(jnp.bfloat16)
    r = jnp.dot(p, values, preferred_element_type=jnp.float32)
    z = jnp.dot(p, jnp.ones((w, LANES), jnp.bfloat16), preferred_element_type=jnp.float32)
    first = lax.broadcasted_iota(jnp.int32, (n, LANES), 1) < LANES // 2
    parts = []
    for hp in range(feats // LANES):
        a = slice(2 * hp * n, (2 * hp + 1) * n)
        b = slice((2 * hp + 1) * n, (2 * hp + 2) * n)
        ls = slice(hp * LANES, (hp + 1) * LANES)
        wide = jnp.where(
            first, jnp.broadcast_to(m[a], (n, LANES)), jnp.broadcast_to(m[b], (n, LANES))
        )
        parts.append((wide, jnp.where(first, z[a], z[b]), jnp.where(first, r[a, ls], r[b, ls])))
    return parts


def merge(one, two):
    top = jnp.maximum(one[0], two[0])
    a = jnp.exp(one[0] - top)
    b = jnp.exp(two[0] - top)
    return top, a * one[1] + b * two[1], a * one[2] + b * two[2]


def kernel(plan, names, *refs):
    R = dict(zip(names, refs))
    q_ref, k_ref, v_ref, out_ref = R["q"], R["k"], R["v"], R["out"]
    feats, length = plan.features, plan.length
    half = BLOCK // 2
    pos = lax.axis_index("seqa") * plan.inner + lax.axis_index("seqb")
    core = lax.rem(pos, 2)
    other = 1 - core
    chip = lax.div(pos, 2)
    has_left = pos > 0
    has_right = pos < plan.devices - 1

    def device(p):
        return (lax.div(p, plan.inner), lax.rem(p, plan.inner))

    sibling = device(2 * chip + other)

    barrier = pltpu.get_barrier_semaphore()
    bits = plan.chips.bit_length() - 1

    def across(i):
        mask = 2**i
        flipped = jnp.where(lax.rem(lax.div(chip, mask), 2) == 1, chip - mask, chip + mask)
        return device(2 * flipped + core)

    far = jnp.where(core == 0, pos - 1, pos + 1)
    has_far = (far >= 0) & (far < plan.devices)
    pl.semaphore_signal(barrier, inc=1, device_id=sibling, device_id_type=MESH)

    @pl.when(has_far)
    def _():
        pl.semaphore_signal(barrier, inc=1, device_id=device(far), device_id_type=MESH)

    for i in range(bits):
        pl.semaphore_signal(barrier, inc=1, device_id=across(i), device_id_type=MESH)

    def tell(i):
        if i < bits:
            pl.semaphore_signal(R["go"].at[i], inc=1, device_id=across(i), device_id_type=MESH)

    def hear(i):
        if i < bits:
            pl.semaphore_wait(R["go"].at[i], 1)

    facts = {}
    for l in plan.deep:
        span = 2 ** (l - 1)
        J = lax.div(pos, span)
        b = jnp.where(lax.rem(pos, span) >= span // 2, 1, 0)
        left_ok = J > 0
        right_ok = J < plan.blocks(l) - 1
        mid_ok = jnp.where(b == 1, J, plan.blocks(l) - 1 - J) > 0
        facts[l] = (J, b, left_ok, right_ok, (left_ok, mid_ok, right_ok))
        buf = R[f"buf{l}"]
        for slot in range(3):
            @pl.when(jnp.logical_not(facts[l][4][slot]))
            def _(buf=buf, slot=slot, l=l):
                if l == 2:
                    buf[slot] = jnp.zeros(buf.shape[1:], buf.dtype)
                else:
                    for c in range(2):
                        buf[c, slot] = jnp.zeros(buf.shape[2:], buf.dtype)

    near = R["near"]

    @pl.when(jnp.logical_not(has_left))
    def _():
        R["fk"][0] = jnp.zeros((BLOCK, feats), jnp.bfloat16)
        R["fv"][0] = jnp.zeros((BLOCK, feats), jnp.bfloat16)
        near[0:half] = jnp.zeros((half, 2 * feats), jnp.bfloat16)

    @pl.when(jnp.logical_not(has_right))
    def _():
        R["fk"][1] = jnp.zeros((BLOCK, feats), jnp.bfloat16)
        R["fv"][1] = jnp.zeros((BLOCK, feats), jnp.bfloat16)
        near[3 * half :] = jnp.zeros((half, 2 * feats), jnp.bfloat16)

    pl.semaphore_wait(barrier, bits + 1 + jnp.where(has_far, 1, 0))
    tell(0)

    def remote(src, dst, send_sem, recv_sem, target):
        return pltpu.make_async_remote_copy(
            src_ref=src, dst_ref=dst, send_sem=send_sem, recv_sem=recv_sem,
            device_id=target, device_id_type=MESH,
        )

    def neighbour_copies(act, which):
        send1 = R["send1"]
        fs, fr = R["fs"], R["fr"]
        for side, step, ok in (
            (0, 1, has_right & (core == 1)),
            (1, -1, has_left & (core == 0)),
            (0, 1, core == 0),
            (1, -1, core == 1),
        ):
            @pl.when(ok)
            def _(side=side, step=step):
                t = device(pos + step)
                base = 3 * side
                for i in which:
                    if i < 2:
                        src = (k_ref, v_ref)[i].at[pl.ds(BLOCK * (1 - side), BLOCK)]
                        dst = R[("fk", "fv")[i]].at[side]
                    else:
                        src = send1.at[pl.ds(half * side, half)]
                        dst = near.at[pl.ds(3 * half * side, half)]
                    act(remote(src, dst, fs.at[base + i], fr.at[base + i], t))

    neighbour_copies(lambda copy: copy.start(), (0, 1))

    pool = jnp.concatenate(
        [pool_matrix(plan.padded[l], length, 2**l) for l in plan.levels], axis=0
    ).astype(jnp.bfloat16)
    R["qp"][...] = jnp.dot(pool, q_ref[...], preferred_element_type=jnp.float32) * 0.125
    tops = {}
    for ref, at in ((k_ref, 0), (v_ref, feats)):
        pooled = jnp.dot(pool, ref[...], preferred_element_type=jnp.float32)
        for l in plan.levels:
            part = pooled[plan.offset[l] : plan.offset[l] + plan.padded[l]]
            send = R[f"send{l}"]
            if plan.packed(l):
                tops.setdefault(l, []).append(part)
            else:
                send[:, at : at + feats] = part.astype(jnp.bfloat16)
    for l, parts in tops.items():
        R[f"send{l}"][...] = jnp.concatenate(parts, axis=0).astype(jnp.bfloat16)

    neighbour_copies(lambda copy: copy.start(), (2,))

    def lanes(hp, base=0):
        return pl.ds(pl.multiple_of(base + hp * LANES, LANES), LANES)

    def own(hp, carry):
        ls = lanes(hp)
        q = q_ref[:, ls].astype(jnp.float32) * 0.125
        m, z, o = attend(q, k_ref[:, ls], v_ref[:, ls], None)
        R["fine"][0, :, ls] = m
        R["fine"][1, :, ls] = z
        R["fine"][2, :, ls] = o
        return carry

    parts = 3
    for i in range(parts):
        hear(i)
        tell(i + 1)
        low, high = i * plan.pairs // parts, (i + 1) * plan.pairs // parts
        lax.fori_loop(low, high, own, 0, unroll=True)
    for i in range(parts, bits):
        hear(i)
        tell(i + 1)

    def deep_copies(l, t, act):
        J, b, left_ok, right_ok, _ = facts[l]
        send, buf = R[f"send{l}"], R[f"buf{l}"]
        ss, rs = R[f"ss{l}"], R[f"rs{l}"]
        if l == 2:
            group, mine, a = 1, 0, core
            ok_r = right_ok & (core == 0)
            ok_l = left_ok & (core == 1)
        else:
            m = plan.half_chips(l)
            group = 2 * m
            mine = lax.rem(chip, m)
            a = jnp.where(t >= m, 1, 0)
            ok_r = right_ok & (a >= b)
            ok_l = left_ok & (a <= b)
        for side, ok, step in ((0, ok_r, 1), (1, ok_l, -1)):
            slot = b + side
            dst = buf.at[slot] if l == 2 else buf.at[core, slot, mine]

            @pl.when(ok)
            def _(side=side, step=step, slot=slot, dst=dst):
                target = device(2 * ((J + step) * group + t) + core)
                act(remote(send, dst, ss.at[side, t], rs.at[slot], target))

    def all_deep(act):
        for l in plan.deep:
            if l == 2:
                deep_copies(l, 0, act)
            else:
                def body(t, carry, l=l):
                    deep_copies(l, t, act)
                    return carry

                lax.fori_loop(0, 2 * plan.half_chips(l), body, 0)

    all_deep(lambda copy: copy.start())

    def arrived(ref, sem):
        pltpu.make_async_copy(ref, ref, sem).wait()

    def relay(l, slot):
        buf = R[f"buf{l}"]
        ys, yr = R[f"ys{l}"].at[slot], R[f"yr{l}"].at[slot]
        if l == 2:
            src = R["stage"] if slot == 1 else buf.at[slot]
            return remote(src, buf.at[slot], ys, yr, sibling)
        return remote(buf.at[core, slot], buf.at[core, slot], ys, yr, sibling)

    def relays_out(l):
        ok = facts[l][4]
        if l == 2:
            return ((0, ok[0] & (core == 0)), (1, has_far), (2, ok[2] & (core == 1)))
        return tuple((slot, ok[slot]) for slot in range(3))

    def relays_in(l):
        ok = facts[l][4]
        if l == 2:
            return ((0, ok[0] & (core == 1)), (1, ok[1]), (2, ok[2] & (core == 0)))
        return tuple((slot, ok[slot]) for slot in range(3))

    def pass_on(l):
        buf = R[f"buf{l}"]
        for slot, ok in relays_out(l):
            if l == 2 and slot == 1:
                continue

            @pl.when(ok)
            def _(slot=slot):
                mine = buf.at[slot] if l == 2 else buf.at[core, slot]
                arrived(mine, R[f"rs{l}"].at[slot])
                relay(l, slot).start()

    def received(l):
        buf = R[f"buf{l}"]
        for slot, ok in relays_in(l):
            @pl.when(ok)
            def _(slot=slot):
                theirs = buf.at[slot] if l == 2 else buf.at[other, slot]
                arrived(theirs, R[f"yr{l}"].at[slot])

    @pl.when(has_left)
    def _():
        arrived(R["fk"].at[0], R["fr"].at[0])
        arrived(R["fv"].at[0], R["fr"].at[1])
        arrived(near.at[pl.ds(0, half)], R["fr"].at[2])

    @pl.when(has_right)
    def _():
        arrived(R["fk"].at[1], R["fr"].at[3])
        arrived(R["fv"].at[1], R["fr"].at[4])
        arrived(near.at[pl.ds(3 * half, half)], R["fr"].at[5])

    pool1 = pool_matrix(half, BLOCK, 2).astype(jnp.bfloat16)
    for side in range(2):
        for name, at in (("fk", 0), ("fv", feats)):
            part = jnp.dot(pool1, R[name][side], preferred_element_type=jnp.float32)
            near[half * (1 + side) : half * (2 + side), at : at + feats] = part.astype(jnp.bfloat16)

    near_at = pl.ds(pl.multiple_of(core * 3 * half, half), half)
    quart = half // 2
    pool4 = pool_matrix(quart, BLOCK, 4).astype(jnp.bfloat16)
    pool2 = pool_matrix(quart, half, 2).astype(jnp.bfloat16)
    for name, at in (("fk", 0), ("fv", feats)):
        fine_part = jnp.dot(pool4, R[name][core], preferred_element_type=jnp.float32)
        near_part = jnp.dot(pool2, near[near_at, at : at + feats], preferred_element_type=jnp.float32)
        for part, place in ((near_part, core), (fine_part, other)):
            rows = pl.ds(pl.multiple_of(place * quart, quart), quart)
            R["stage"][rows, at : at + feats] = part.astype(jnp.bfloat16)

    @pl.when(has_far)
    def _():
        relay(2, 1).start()

    gone_left = jnp.where(has_left, 0.0, NEVER).astype(jnp.float32)
    gone_right = jnp.where(has_right, 0.0, NEVER).astype(jnp.float32)
    row = lax.broadcasted_iota(jnp.int32, (BLOCK, 2 * BLOCK), 0)
    col = lax.broadcasted_iota(jnp.int32, (BLOCK, 2 * BLOCK), 1)
    upper = row >= half
    quarter = col // half
    hidden = (upper & (quarter == 2)) | (jnp.logical_not(upper) & (quarter == 1))
    R["bias"][...] = jnp.where(hidden, NEVER, 0.0) + jnp.where(quarter < 2, gone_left, gone_right)

    def beside(hp, carry):
        ls = lanes(hp)
        vs = lanes(hp, feats)
        fine = R["fine"]
        for side, gone in ((0, gone_left), (1, gone_right)):
            rows = slice(side * BLOCK, (side + 1) * BLOCK)
            q = q_ref[rows, ls].astype(jnp.float32) * 0.125
            m, z, o = attend(q, R["fk"][side, :, ls], R["fv"][side, :, ls], None)
            m = m + gone
            both = merge((m, z, o), (fine[0, rows, ls], fine[1, rows, ls], fine[2, rows, ls]))
            for i in range(3):
                fine[i, rows, ls] = both[i]
        m, z, o = attend(R["qp"][0:BLOCK, ls], near[:, ls], near[:, vs], R["bias"][...])
        R["terms1"][0, :, ls] = m + LOG_TWO
        R["terms1"][1, :, ls] = z
        R["terms1"][2, :, ls] = o
        return carry

    lax.fori_loop(0, plan.pairs, beside, 0, unroll=True)

    def key_count(l):
        return 3 * plan.padded[l] * (1 if l == 2 else 2 * plan.half_chips(l))

    def deep_bias(l):
        width = key_count(l)
        per_slot = plan.padded[l] * (1 if l == 2 else plan.half_chips(l))
        c = lax.broadcasted_iota(jnp.int32, (1, width), 1)
        slot = lax.rem(c // per_slot, 3)
        gone = [jnp.where(ok, 0.0, NEVER).astype(jnp.float32) for ok in facts[l][4]]
        bias = jnp.where(slot == 0, gone[0], jnp.where(slot == 1, gone[1], gone[2]))
        if plan.rows[l] < plan.padded[l]:
            bias = jnp.where(lax.rem(c, plan.padded[l]) < plan.rows[l], bias, NEVER)
        return bias

    def deep_level(l):
        bias = deep_bias(l)
        buf = R[f"buf{l}"]
        width = key_count(l)
        at = (slice(None),) * (len(buf.shape) - 1)

        def body(hp, carry):
            ls = lanes(hp)
            if plan.packed(l):
                block = buf[at + (ls,)].astype(jnp.float32)
                keys = block[:, :, :, :8].reshape(width, LANES).astype(jnp.bfloat16)
                values = block[:, :, :, 8:].reshape(width, LANES).astype(jnp.bfloat16)
            else:
                keys = buf[at + (ls,)].reshape(width, LANES)
                values = buf[at + (lanes(hp, feats),)].reshape(width, LANES)
            q = R["qp"][plan.offset[l] : plan.offset[l] + plan.padded[l], ls]
            m, z, o = attend(q, keys, values, bias)
            R[f"terms{l}"][0, :, ls] = m + l * LOG_TWO
            R[f"terms{l}"][1, :, ls] = z
            R[f"terms{l}"][2, :, ls] = o
            return carry

        if plan.padded[l] > ALL_HEADS_ROWS:
            lax.fori_loop(0, plan.pairs, body, 0, unroll=True)
            return
        if plan.packed(l):
            block = buf[...].astype(jnp.float32)
            keys = block[:, :, :, :8].reshape(width, feats).astype(jnp.bfloat16)
            values = block[:, :, :, 8:].reshape(width, feats).astype(jnp.bfloat16)
        else:
            keys = buf[at + (slice(0, feats),)].reshape(width, feats)
            values = buf[at + (slice(feats, 2 * feats),)].reshape(width, feats)
        q = R["qp"][plan.offset[l] : plan.offset[l] + plan.padded[l], :]
        for hp, (m, z, o) in enumerate(attend_all(q, keys, values, bias)):
            ls = slice(hp * LANES, (hp + 1) * LANES)
            R[f"terms{l}"][0, :, ls] = m + l * LOG_TWO
            R[f"terms{l}"][1, :, ls] = z
            R[f"terms{l}"][2, :, ls] = o

    for l in plan.deep:
        pass_on(l)
    for l in plan.deep:
        received(l)
        deep_level(l)

    def last(hp, carry):
        ls = lanes(hp)

        def widen(l, terms):
            wide = R[f"wide{l}"]
            n = terms[0].shape[0]
            for i in range(3):
                view = wide.at[hp, i]
                view[pl.ds(0, n, stride=2), :] = terms[i]
                view[pl.ds(1, n, stride=2), :] = terms[i]
            keep = length if l == 1 else plan.padded[l - 1]
            return tuple(wide[hp, i][:keep] for i in range(3))

        current = None
        for l in reversed(plan.levels):
            terms = tuple(R[f"terms{l}"][i, :, ls] for i in range(3))
            current = terms if current is None else merge(current, terms)
            current = widen(l, current)
        fine = tuple(R["fine"][i, :, ls] for i in range(3))
        _, z, o = merge(current, fine)
        out_ref[:, ls] = (o / z).astype(jnp.bfloat16)
        return carry

    lax.fori_loop(0, plan.pairs, last, 0, unroll=True)

    all_deep(lambda copy: copy.wait_send())
    neighbour_copies(lambda copy: copy.wait_send(), (0, 1, 2))
    for l in plan.deep:
        for slot, ok in relays_out(l):
            @pl.when(ok)
            def _(l=l, slot=slot):
                relay(l, slot).wait_send()


def shards(plan, q, k, v):
    f, length = plan.features, plan.length
    scratch = {}
    scratch["qp"] = pltpu.VMEM((plan.pooled_rows, f), jnp.float32)
    sem = pltpu.SemaphoreType.DMA
    for l in plan.levels:
        link = plan.link_shape(l)
        scratch[f"send{l}"] = pltpu.VMEM(link, jnp.bfloat16)
        scratch[f"terms{l}"] = pltpu.VMEM((3, plan.padded[l], f), jnp.float32)
        if l == 1:
            continue
        if l == 2:
            scratch["buf2"] = pltpu.VMEM((3,) + link, jnp.bfloat16)
            scratch["stage"] = pltpu.VMEM(link, jnp.bfloat16)
            scratch["ss2"] = sem((2, 1))
        else:
            m = plan.half_chips(l)
            scratch[f"buf{l}"] = pltpu.VMEM((2, 3, m) + link, jnp.bfloat16)
            scratch[f"ss{l}"] = sem((2, 2 * m))
        scratch[f"rs{l}"] = sem((3,))
        scratch[f"ys{l}"] = sem((3,))
        scratch[f"yr{l}"] = sem((3,))
    scratch["fk"] = pltpu.VMEM((2, BLOCK, f), jnp.bfloat16)
    scratch["fv"] = pltpu.VMEM((2, BLOCK, f), jnp.bfloat16)
    scratch["near"] = pltpu.VMEM((2 * BLOCK, 2 * f), jnp.bfloat16)
    scratch["go"] = pltpu.SemaphoreType.REGULAR((max(1, plan.chips.bit_length() - 1),))
    scratch["fs"] = pltpu.SemaphoreType.DMA((6,))
    scratch["fr"] = pltpu.SemaphoreType.DMA((6,))
    scratch["fine"] = pltpu.VMEM((3, length, f), jnp.float32)
    scratch["bias"] = pltpu.VMEM((BLOCK, 2 * BLOCK), jnp.float32)
    for l in plan.levels:
        scratch[f"wide{l}"] = pltpu.VMEM((plan.pairs, 3, 2 * plan.padded[l], LANES), jnp.float32)
    names = ["q", "k", "v", "out"] + list(scratch)
    return pl.pallas_call(
        functools.partial(kernel, plan, names),
        out_shape=jax.ShapeDtypeStruct((length, f), jnp.bfloat16),
        in_specs=[pl.BlockSpec(memory_space=pltpu.VMEM)] * 3,
        out_specs=pl.BlockSpec(memory_space=pltpu.VMEM),
        scratch_shapes=list(scratch.values()),
        compiler_params=pltpu.CompilerParams(
            collective_id=0, has_side_effects=True, vmem_limit_bytes=56 * 2**20
        ),
        name="hier_attention",
    )(q, k, v)


def solution(mesh):
    outer, inner = mesh.shape["seqa"], mesh.shape["seqb"]
    spec = P(("seqa", "seqb"), None)

    def part(q, k, v):
        plan = Plan(q.shape[0], q.shape[1], outer, inner)
        return shards(plan, q, k, v)

    return jax.shard_map(part, mesh=mesh, in_specs=(spec,) * 3, out_specs=spec, check_vma=False)
```
